32 devices in a mesh: expert: 8 (over z, core), dp: 4 (over y, x).
Axes of the slice: x: 2, y: 2, z: 4, core: 2. Of those that a mesh axis runs over, the one named last changes fastest.
Arguments:
- tokens: bfloat16 [4096, 2048], P(('expert', 'dp')), may hold values from -6 to 6
- cotangent: bfloat16 [4096, 2048], P(('expert', 'dp')), may hold values from -6 to 6
- gates: float32 [4096, 2], P(('expert', 'dp')), may hold values from 0.2 to 1
- expert_ids: int32 [4096, 2], P(('expert', 'dp')), may hold values from 0 to 7, all different within a row; in each aligned block of 128 rows (0 to 127, 128 to 255, ...) at most 40 rows name the same one
- w_in: bfloat16 [8, 2048, 704], P('expert'), may hold values from -0.125 to 0.125
- w_out: bfloat16 [8, 704, 2048], P('expert'), may hold values from -0.21875 to 0.21875
Outputs:
- grad_tokens: bfloat16 [4096, 2048], P(('expert', 'dp'))
- grad_w_out: bfloat16 [8, 704, 2048], P('expert', None, 'dp')
The draws below stay inside these ranges and needn't reach their ends.
Inputs may be any that keep to these rules, and one draw needn't show every extreme that they name: `expert_ids`: the 2 ids of a token differ. In the rows of one device (aligned blocks of 128 rows), no expert is named more than 40 times.
All inputs are finite; a program needn't handle non-finite values.
Results may differ from the reference program's by a relative error of at most 0.018.
Values may be sent and summed in bfloat16 or wider, within the bound.
A program may use at most 64 MiB of HBM per device.

```python
import math
import jax
import jax.numpy as jnp
import numpy as np
from jax import lax

D = 2048
HW = 704
TOP = 2
TOK_DEV = 128
EXPERTS = 8
CAP = 40
TOKENS = 4096
N_EXPERT = 8
N_DP = 4


def with_spikes(result, rng, source, target, blocks, factor):
    def block_of(axis_at):
        return (jnp.arange(result.shape[axis_at]) // (result.shape[axis_at] // blocks)).reshape((-1,) + (1,) * (result.ndim - 1 - axis_at))

    one_side = jax.random.permutation(rng, blocks)[block_of(target)]
    second = (block_of(target) + blocks // 2) % blocks
    return jnp.where((block_of(source) == one_side) | (block_of(source) == second), factor * result, result)


def shard_levels(own_key, shape, pieces, least, top_value):
    gain, own = 1.0, jax.random.fold_in(own_key, 6)
    for dim, shards_of in pieces:
        heights = jnp.exp(jax.random.uniform(jax.random.fold_in(own, dim), (shards_of,), jnp.float32, least / len(pieces), top_value / len(pieces)))
        gain = gain * jnp.repeat(heights, shape[dim] // shards_of).reshape([-1 if axis == dim else 1 for axis in range(len(shape))])
    return gain


def assign_block(rng, own, number, rows, amount, top, reach, skew):
    sequence = jax.random.permutation(rng, amount)
    packed, usual = shares(amount, rows * top, reach, skew, True), shares(amount, rows * top, reach, skew, False)
    places = jnp.arange(amount)

    def named(lengths, rotation):
        used = int((lengths > 0).sum())
        fixed = max(1, used // 4)
        passed = fixed + (places - fixed + rotation * (used - fixed)) % max(1, amount - fixed)
        return jnp.zeros((amount,), jnp.int32).at[sequence[jnp.where(places < fixed, places, passed)]].set(jnp.asarray(lengths, jnp.int32))

    lengths = jnp.where(number % 4 == 0, named(packed, number // 4), named(usual, number - number // 4 - 1))
    mixed = jax.random.permutation(jax.random.fold_in(own, 3), amount)
    giver, taker = mixed[0:amount // 2 * 2:2], mixed[1:amount // 2 * 2:2]
    slack = jnp.minimum(lengths[giver] - 1, reach - lengths[taker]) // 2
    slack = jnp.where((giver == sequence[0]) | (taker == sequence[0]) | (lengths[taker] == 0), 0, jnp.maximum(slack, 0))
    passed = jax.random.randint(jax.random.fold_in(own, 4), (amount // 2,), 0, 1 << 20) % (slack + 1)
    lengths = lengths.at[giver].add(-passed).at[taker].add(passed)
    members = jnp.searchsorted(jnp.cumsum(lengths), jnp.arange(rows * top), side="right").astype(jnp.int32)
    table = members.reshape(top, rows).T
    table = table[jax.random.permutation(jax.random.fold_in(own, 1), rows)]
    rotation = jax.random.randint(jax.random.fold_in(own, 2), (rows, 1), 0, top)
    return jnp.take_along_axis(table, (jnp.arange(top)[None, :] + rotation) % top, axis=1)


def shares(amount, total, bound, skew, full):
    portions = [(1 << 20) // math.isqrt(standing ** skew) + 1 for standing in range(1, amount + 1)]
    largest = bound if full else min(bound, max(-(-total // amount), total * portions[0] // sum(portions)))
    least = 1 if total - largest >= amount - 1 else 0
    counts, spare = [largest] + [least] * (amount - 1), total - largest - least * (amount - 1)
    while spare > 0:
        movable = [i for i in range(1, amount) if counts[i] < largest] or [i for i in range(1, amount) if counts[i] < bound]
        whole, budget = sum([portions[i] for i in movable]), spare
        for i in movable:
            addition = min(bound - counts[i], max(1, budget * portions[i] // whole), spare)
            counts[i] = counts[i] + addition
            spare = spare - addition
    return np.array(counts)


def bell_draw(key, extent, width, bound, cuts=(), kind=jnp.bfloat16):
    loudness = shard_levels(key, extent, cuts, -0.22, 0.18) if cuts else 1.0
    drawn = jax.random.normal(key, extent, jnp.float32) * width * loudness
    return jnp.minimum(jnp.maximum(drawn, -bound), bound).astype(kind)


def bell_draw_with(key, shape, scale, limit, cuts, heavy, kind=jnp.bfloat16):
    array = scale * jax.random.normal(key, shape, jnp.float32)
    if cuts:
        array = array * shard_levels(key, shape, cuts, -0.22, 0.18)
    return jnp.clip(with_spikes(array, jax.random.fold_in(key, 3), *heavy), -limit, limit).astype(kind)


def setup_inputs(seed: int = 0) -> dict:
    streams_of = jax.random.split(jax.random.key(seed), 7)
    tokens = bell_draw(streams_of[0], (TOKENS, D), 1.0, 6.0, ((0, 32),))
    cotangent = bell_draw_with(streams_of[1], (TOKENS, D), 1.0, 6.0, ((0, 32),), (0, 1, 32, 2.75))
    gates = jnp.clip(0.2 + 0.8 * jax.random.uniform(streams_of[2], (TOKENS, TOP), jnp.float32) ** shard_levels(streams_of[2], (TOKENS, TOP), ((0, 32),), -0.2, 0.2), 0.2, 1.0)
    expert_ids_keys = jax.random.split(jax.random.fold_in(streams_of[3], 1), TOKENS // TOK_DEV)
    expert_ids_turns = jax.random.permutation(jax.random.fold_in(streams_of[3], 3), TOKENS // TOK_DEV)
    expert_ids = jax.vmap(lambda own, number: assign_block(jax.random.fold_in(streams_of[3], 2), own, number, TOK_DEV, EXPERTS, TOP, CAP, 2))(expert_ids_keys, expert_ids_turns).reshape((TOKENS, TOP))
    w_in = bell_draw(streams_of[4], (EXPERTS, D, HW), D ** -0.5, 0.125, ((0, 8),))
    w_out = bell_draw(streams_of[5], (EXPERTS, HW, D), HW ** -0.5, 0.21875, ((0, 8),))
    return dict(tokens=tokens, cotangent=cotangent, gates=gates, expert_ids=expert_ids, w_in=w_in, w_out=w_out)


def reference(tokens, cotangent, gates, expert_ids, w_in, w_out):
    blocks = N_EXPERT * N_DP
    assigns = TOK_DEV * TOP
    flat_ids = expert_ids.reshape(blocks, assigns)
    onehot_table = (flat_ids[:, :, None] == jnp.arange(N_EXPERT, dtype=jnp.int32)[None, None, :]).astype(jnp.int32)
    position = jnp.sum((jnp.cumsum(onehot_table, axis=1) - onehot_table) * onehot_table, axis=2)
    assign_index = jnp.arange(assigns, dtype=jnp.int32)
    token_index = jnp.arange(blocks, dtype=jnp.int32)[:, None] * TOK_DEV + (assign_index // TOP)[None, :]
    gate_flat = gates.reshape(blocks, assigns)
    slot_index = jnp.arange(CAP, dtype=jnp.int32)
    dims_t = (((1,), (1,)), ((), ()))

    def per_expert(carry, expert):
        matches = (flat_ids == expert)[:, None, :] & (position[:, None, :] == slot_index[None, :, None])
        filled = jnp.any(matches, axis=2)
        source = jnp.sum(jnp.where(matches, token_index[:, None, :], 0), axis=2).astype(jnp.int32)
        weight = jnp.sum(jnp.where(matches, gate_flat[:, None, :], jnp.float32(0.0)), axis=2)
        rows_x = jnp.where(filled[..., None], tokens[source], jnp.zeros((), tokens.dtype)).reshape(-1, D)
        rows_dy = jnp.where(filled[..., None], cotangent[source].astype(jnp.float32) * weight[..., None], jnp.float32(0.0)).astype(jnp.bfloat16).reshape(-1, D)
        w_first = w_in[expert]
        w_second = w_out[expert]
        pre_act = jnp.dot(rows_x, w_first, preferred_element_type=jnp.float32)
        sigmoid_pre = jax.nn.sigmoid(pre_act)
        act = (pre_act * sigmoid_pre).astype(jnp.bfloat16)
        back_proj = lax.dot_general(rows_dy, w_second, dims_t, preferred_element_type=jnp.float32)
        dpre_act = (back_proj * sigmoid_pre * (1.0 + pre_act * (1.0 - sigmoid_pre))).astype(jnp.bfloat16)
        grad_rows = lax.dot_general(dpre_act, w_first, dims_t, preferred_element_type=jnp.float32).astype(jnp.bfloat16)
        carry = carry.at[source.reshape(-1)].add(jnp.where(filled.reshape(-1)[:, None], grad_rows.astype(jnp.float32), jnp.float32(0.0)))
        act_groups = act.reshape(N_EXPERT, N_DP, CAP, HW).astype(jnp.float32)
        dy_groups = rows_dy.reshape(N_EXPERT, N_DP, CAP, D).astype(jnp.float32)
        partial_value = jnp.einsum("sgch,sgcd->ghd", act_groups, dy_groups).astype(jnp.bfloat16)
        grad_w = jnp.sum(partial_value.astype(jnp.float32), axis=0).astype(jnp.bfloat16)
        return carry, grad_w

    start_carry = jnp.zeros((TOKENS, D), jnp.float32)
    summed, grad_w_out = lax.scan(per_expert, start_carry, jnp.arange(N_EXPERT, dtype=jnp.int32))
    return summed.astype(jnp.bfloat16), grad_w_out
```

```python
import functools

import jax
import jax.numpy as jnp
from jax import lax
from jax.experimental import pallas as pl
from jax.experimental.pallas import tpu as pltpu
from jax.sharding import PartitionSpec as P

BY_COLS = (((1,), (1,)), ((), ()))
BY_ROWS = (((0,), (0,)), ((), ()))


def layer_kernel(
    experts, groups, tokens, cotangent, gates, ids, w_in_hbm, w_out_hbm, grad_tokens, grad_w,
    w_in, w_out, places, gains, sent_rows, sent_grads, got_rows, got_grads, dpre, sent_back,
    got_back, total, w_total, w_sent, w_got, load_sems, send_sems, recv_sems, w_send, w_recv,
):
    me = lax.axis_index("expert")
    group = lax.axis_index("dp")
    half = experts // 2
    slots = got_rows.shape[1]
    columns = grad_w.shape[1]

    loads = [
        pltpu.make_async_copy(w_in_hbm, w_in, load_sems.at[0]),
        pltpu.make_async_copy(w_out_hbm, w_out, load_sems.at[1]),
    ]
    for load in loads:
        load.start()

    barrier = pltpu.get_barrier_semaphore()

    def greet_expert(step, carry):
        pl.semaphore_signal(barrier, inc=1, device_id={"expert": (me + step) % experts})
        return carry

    def greet_group(step, carry):
        pl.semaphore_signal(barrier, inc=1, device_id={"dp": (group + step) % groups})
        return carry

    lax.fori_loop(1, experts, greet_expert, 0)
    lax.fori_loop(1, groups, greet_group, 0)

    my_half = me // half
    other = (1 - my_half) * half

    def target(step):
        return jnp.where(
            step < half, other + (me + step) % half, my_half * half + (me + step - half + 1) % half
        )

    def origin(step):
        return jnp.where(
            step < half,
            other + (me + half - step % half) % half,
            my_half * half + (me + 2 * half - step % half - 1) % half,
        )

    def exchange(kind, source, dest, peer, here, there):
        return pltpu.make_async_remote_copy(
            src_ref=source.at[here],
            dst_ref=dest.at[there],
            send_sem=send_sems.at[kind, here],
            recv_sem=recv_sems.at[kind, there],
            device_id={"expert": peer},
        )

    rows = tokens.shape[0]
    expert_of = lax.broadcasted_iota(jnp.int32, (experts, rows), 0)
    chosen = jnp.zeros((experts, rows), jnp.float32)
    gain = jnp.zeros((experts, rows), jnp.float32)
    for k in range(ids.shape[0]):
        hit = expert_of == ids[k : k + 1, :]
        chosen = chosen + jnp.where(hit, 1.0, 0.0)
        gain = gain + jnp.where(hit, gates[k : k + 1, :], 0.0)
    earlier = jnp.where(
        lax.broadcasted_iota(jnp.int32, (rows, rows), 0)
        < lax.broadcasted_iota(jnp.int32, (rows, rows), 1),
        1.0,
        0.0,
    ).astype(jnp.bfloat16)
    place = jnp.dot(chosen.astype(jnp.bfloat16), earlier, preferred_element_type=jnp.float32)
    places[...] = jnp.where(chosen > 0.0, place, -1.0)
    gains[...] = gain
    slot_number = lax.broadcasted_iota(jnp.int32, (slots, rows), 0).astype(jnp.float32)

    def choose(expert):
        return slot_number == places[pl.ds(expert, 1), :]

    def pack(expert, rows_to, grads_to):
        match = choose(expert)
        pick = jnp.where(match, 1.0, 0.0).astype(jnp.bfloat16)
        weight = jnp.sum(jnp.where(match, gains[pl.ds(expert, 1), :], 0.0), axis=1, keepdims=True)
        picked = jnp.dot(pick, tokens[...], preferred_element_type=jnp.float32)
        rows_to[expert] = picked.astype(jnp.bfloat16)
        gated = jnp.dot(pick, cotangent[...], preferred_element_type=jnp.float32) * weight
        grads_to[expert] = gated.astype(jnp.bfloat16)

    pl.semaphore_wait(barrier, experts + groups - 2)

    def dispatch(step, carry):
        to = target(step)
        pack(to, sent_rows, sent_grads)
        exchange(0, sent_rows, got_rows, to, to, me).start()
        exchange(1, sent_grads, got_grads, to, to, me).start()
        return carry

    lax.fori_loop(0, experts - 1, dispatch, 0)
    pack(me, got_rows, got_grads)
    w_total[...] = jnp.zeros_like(w_total)
    for load in loads:
        load.wait()

    def absorb(source):
        x = got_rows[source]
        dy = got_grads[source]
        pre = lax.dot_general(x, w_in[...], BY_COLS, preferred_element_type=jnp.float32)
        sig = 1.0 / (1.0 + jnp.exp(-pre))
        act = (pre * sig).astype(jnp.bfloat16)
        for g in range(groups):
            w_total[g] += lax.dot_general(
                act,
                dy[:, g * columns : (g + 1) * columns],
                BY_ROWS,
                preferred_element_type=jnp.float32,
            )
        back = lax.dot_general(dy, w_out[...], BY_COLS, preferred_element_type=jnp.float32)
        dpre[source] = (back * sig * (1.0 + pre * (1.0 - sig))).astype(jnp.bfloat16)

    absorb(me)

    def receive(step, carry):
        source = origin(step)
        exchange(0, sent_rows, got_rows, source, source, source).wait_recv()
        exchange(1, sent_grads, got_grads, source, source, source).wait_recv()
        absorb(source)
        return carry

    lax.fori_loop(0, experts - 1, receive, 0)

    def share(to, slot):
        return pltpu.make_async_remote_copy(
            src_ref=w_sent.at[to],
            dst_ref=w_got.at[slot],
            send_sem=w_send.at[to],
            recv_sem=w_recv.at[slot],
            device_id={"dp": to},
        )

    def spread(step, carry):
        to = (group + step) % groups
        w_sent[to] = w_total[to].astype(jnp.bfloat16)
        share(to, group).start()
        return carry

    lax.fori_loop(1, groups, spread, 0)

    def rows_of(source):
        return jnp.dot(dpre[source], w_in[...], preferred_element_type=jnp.float32).astype(
            jnp.bfloat16
        )

    def give_back(step, carry):
        to = target(step)
        sent_back[to] = rows_of(to)
        exchange(2, sent_back, got_back, to, to, me).start()
        return carry

    lax.fori_loop(0, experts - 1, give_back, 0)
    got_back[me] = rows_of(me)

    def combine(source):
        pick = jnp.where(choose(source), 1.0, 0.0).astype(jnp.bfloat16)
        return lax.dot_general(pick, got_back[source], BY_ROWS, preferred_element_type=jnp.float32)

    total[...] = combine(me)

    def take_back(step, carry):
        source = origin(step)
        exchange(2, sent_back, got_back, source, source, source).wait_recv()
        total[...] += combine(source)
        return carry

    lax.fori_loop(0, experts - 1, take_back, 0)
    grad_tokens[...] = total[...].astype(jnp.bfloat16)

    w_total[group] = w_total[group].astype(jnp.bfloat16).astype(jnp.float32)

    def gather(step, carry):
        source = (group + step) % groups
        share(source, source).wait_recv()
        w_total[group] += w_got[source].astype(jnp.float32)
        return carry

    lax.fori_loop(1, groups, gather, 0)
    grad_w[...] = w_total[group].astype(jnp.bfloat16)

    def drain(step, carry):
        to = target(step)
        exchange(0, sent_rows, got_rows, to, to, me).wait_send()
        exchange(1, sent_grads, got_grads, to, to, me).wait_send()
        exchange(2, sent_back, got_back, to, to, me).wait_send()
        return carry

    def drain_group(step, carry):
        share((group + step) % groups, group).wait_send()
        return carry

    lax.fori_loop(0, experts - 1, drain, 0)
    lax.fori_loop(1, groups, drain_group, 0)


def per_device(tokens, cotangent, gates, expert_ids, w_in, w_out):
    rows, width = tokens.shape
    hidden = w_out.shape[1]
    experts, groups = lax.axis_size("expert"), lax.axis_size("dp")
    capacity = 5 * rows * expert_ids.shape[1] // (4 * experts)
    slots = -(-capacity // 8) * 8
    columns = width // groups
    blocks = pltpu.VMEM((experts, slots, width), jnp.bfloat16)
    shares = pltpu.VMEM((groups, hidden, columns), jnp.bfloat16)
    vmem = pl.BlockSpec(memory_space=pltpu.VMEM)
    anywhere = pl.BlockSpec(memory_space=pl.ANY)
    multiplies = experts * slots * width * hidden
    grad_tokens, grad_w = pl.pallas_call(
        functools.partial(layer_kernel, experts, groups),
        out_shape=(
            jax.ShapeDtypeStruct((rows, width), jnp.bfloat16),
            jax.ShapeDtypeStruct((hidden, columns), jnp.bfloat16),
        ),
        in_specs=[vmem] * 4 + [anywhere] * 2,
        out_specs=(vmem, vmem),
        scratch_shapes=[
            pltpu.VMEM((hidden, width), jnp.bfloat16),
            pltpu.VMEM((hidden, width), jnp.bfloat16),
            pltpu.VMEM((experts, rows), jnp.float32),
            pltpu.VMEM((experts, rows), jnp.float32),
            blocks,
            blocks,
            blocks,
            blocks,
            pltpu.VMEM((experts, slots, hidden), jnp.bfloat16),
            blocks,
            blocks,
            pltpu.VMEM((rows, width), jnp.float32),
            pltpu.VMEM((groups, hidden, columns), jnp.float32),
            shares,
            shares,
            pltpu.SemaphoreType.DMA((2,)),
            pltpu.SemaphoreType.DMA((3, experts)),
            pltpu.SemaphoreType.DMA((3, experts)),
            pltpu.SemaphoreType.DMA((groups,)),
            pltpu.SemaphoreType.DMA((groups,)),
        ],
        compiler_params=pltpu.CompilerParams(
            collective_id=0, has_side_effects=True, vmem_limit_bytes=56 * 1024 * 1024
        ),
        cost_estimate=pl.CostEstimate(
            flops=8 * multiplies, bytes_accessed=4 * hidden * width, transcendentals=0
        ),
    )(
        tokens,
        cotangent,
        gates.T,
        expert_ids.T,
        jnp.swapaxes(w_in[0], 0, 1),
        w_out[0],
    )
    return grad_tokens, grad_w[None]


def solution(mesh):
    split = P(("expert", "dp"), None)
    whole = P("expert", None, None)
    return jax.shard_map(
        per_device,
        mesh=mesh,
        in_specs=(split, split, split, split, whole, whole),
        out_specs=(split, P("expert", None, "dp")),
        check_vma=False,
    )
```

```python
import functools

import jax
import jax.numpy as jnp
from jax import lax
from jax.experimental import pallas as pl
from jax.experimental.pallas import tpu as pltpu
from jax.sharding import PartitionSpec as P

BY_COLS = (((1,), (1,)), ((), ()))
BY_ROWS = (((0,), (0,)), ((), ()))


def layer_kernel(
    experts, groups, pieces, tokens, cotangent, gates, ids, w_in_hbm, w_out_hbm, grad_tokens,
    grad_w, w_in, w_out, places, gains, sent_rows, sent_grads, got_rows, got_grads, act, slope,
    back, sent_back, got_back, total, w_own, w_sent, w_got, load_sems, row_send, row_recv,
    grad_send, grad_recv, back_send, back_recv, w_send, w_recv,
):
    me = lax.axis_index("expert")
    group = lax.axis_index("dp")
    half = experts // 2
    slots = got_rows.shape[1]
    columns = grad_w.shape[1]
    per_piece = groups // pieces
    width = per_piece * columns
    my_piece = group // per_piece

    loads = [pltpu.make_async_copy(w_in_hbm, w_in, load_sems.at[pieces])] + [
        pltpu.make_async_copy(
            w_out_hbm.at[:, pl.ds(p * width, width)], w_out.at[p], load_sems.at[p]
        )
        for p in range(pieces)
    ]
    for load in loads:
        load.start()

    barrier = pltpu.get_barrier_semaphore()

    def greet_expert(step, carry):
        pl.semaphore_signal(barrier, inc=1, device_id={"expert": (me + step) % experts})
        return carry

    def greet_group(step, carry):
        pl.semaphore_signal(barrier, inc=1, device_id={"dp": (group + step) % groups})
        return carry

    lax.fori_loop(1, experts, greet_expert, 0)
    lax.fori_loop(1, groups, greet_group, 0)

    my_half = me // half
    other = (1 - my_half) * half

    def target(step):
        return jnp.where(
            step < half, other + (me + step) % half, my_half * half + (me + step - half + 1) % half
        )

    def origin(step):
        return jnp.where(
            step < half,
            other + (me + half - step % half) % half,
            my_half * half + (me + 2 * half - step % half - 1) % half,
        )

    def piece_of(turn):
        return (my_piece + 1 + turn) % pieces

    def rows_copy(to, here, there):
        return pltpu.make_async_remote_copy(
            src_ref=sent_rows.at[here],
            dst_ref=got_rows.at[there],
            send_sem=row_send.at[here],
            recv_sem=row_recv.at[there],
            device_id={"expert": to},
        )

    def grads_copy(piece, to, here, there):
        return pltpu.make_async_remote_copy(
            src_ref=sent_grads.at[piece, here],
            dst_ref=got_grads.at[piece, there],
            send_sem=grad_send.at[piece, here],
            recv_sem=grad_recv.at[piece, there],
            device_id={"expert": to},
        )

    def back_copy(to, here, there):
        return pltpu.make_async_remote_copy(
            src_ref=sent_back.at[here],
            dst_ref=got_back.at[there],
            send_sem=back_send.at[here],
            recv_sem=back_recv.at[there],
            device_id={"expert": to},
        )

    rows = tokens.shape[0]
    expert_of = lax.broadcasted_iota(jnp.int32, (experts, rows), 0)
    chosen = jnp.zeros((experts, rows), jnp.float32)
    gain = jnp.zeros((experts, rows), jnp.float32)
    for k in range(ids.shape[0]):
        hit = expert_of == ids[k : k + 1, :]
        chosen = chosen + jnp.where(hit, 1.0, 0.0)
        gain = gain + jnp.where(hit, gates[k : k + 1, :], 0.0)
    earlier = jnp.where(
        lax.broadcasted_iota(jnp.int32, (rows, rows), 0)
        < lax.broadcasted_iota(jnp.int32, (rows, rows), 1),
        1.0,
        0.0,
    ).astype(jnp.bfloat16)
    place = jnp.dot(chosen.astype(jnp.bfloat16), earlier, preferred_element_type=jnp.float32)
    places[...] = jnp.where(chosen > 0.0, place, -1.0)
    gains[...] = gain
    slot_number = lax.broadcasted_iota(jnp.int32, (slots, rows), 0).astype(jnp.float32)

    def choose(expert):
        return slot_number == places[pl.ds(expert, 1), :]

    def pack_rows(expert, into):
        pick = jnp.where(choose(expert), 1.0, 0.0).astype(jnp.bfloat16)
        picked = jnp.dot(pick, tokens[...], preferred_element_type=jnp.float32)
        into[expert] = picked.astype(jnp.bfloat16)

    def pack_grads(piece, expert, into):
        match = choose(expert)
        pick = jnp.where(match, 1.0, 0.0).astype(jnp.bfloat16)
        weight = jnp.sum(jnp.where(match, gains[pl.ds(expert, 1), :], 0.0), axis=1, keepdims=True)
        part = cotangent[:, pl.ds(pl.multiple_of(piece * width, width), width)]
        gated = jnp.dot(pick, part, preferred_element_type=jnp.float32) * weight
        into[piece, expert] = gated.astype(jnp.bfloat16)

    pl.semaphore_wait(barrier, experts + groups - 2)

    def send_rows(step, carry):
        to = target(step)
        pack_rows(to, sent_rows)
        rows_copy(to, to, me).start()
        return carry

    def send_grads(turn, step):
        to = target(step)
        piece = piece_of(turn)
        pack_grads(piece, to, sent_grads)
        grads_copy(piece, to, to, me).start()

    def send_first_grads(step, carry):
        send_grads(0, step)
        return carry

    lax.fori_loop(0, experts - 1, send_rows, 0)
    lax.fori_loop(0, experts - 1, send_first_grads, 0)
    pack_rows(me, got_rows)
    for p in range(pieces):
        pack_grads(p, me, got_grads)
    for load in loads:
        load.wait()

    def absorb_rows(source):
        pre = lax.dot_general(
            got_rows[source], w_in[...], BY_COLS, preferred_element_type=jnp.float32
        )
        sig = 1.0 / (1.0 + jnp.exp(-pre))
        act[source] = (pre * sig).astype(jnp.bfloat16)
        slope[source] = sig * (1.0 + pre * (1.0 - sig))

    def take_rows(step, carry):
        source = origin(step)
        rows_copy(source, source, source).wait_recv()
        absorb_rows(source)
        if pieces > 1:
            send_grads(1, step)
        return carry

    absorb_rows(me)
    lax.fori_loop(0, experts - 1, take_rows, 0)

    def back_part(piece, source):
        return lax.dot_general(
            got_grads[piece, source], w_out[piece], BY_COLS, preferred_element_type=jnp.float32
        )

    def give_back(source, into, done):
        dpre = (done * slope[source]).astype(jnp.bfloat16)
        into[source] = jnp.dot(dpre, w_in[...], preferred_element_type=jnp.float32).astype(
            jnp.bfloat16
        )

    def share(to, slot):
        return pltpu.make_async_remote_copy(
            src_ref=w_sent.at[to],
            dst_ref=w_got.at[slot],
            send_sem=w_send.at[to],
            recv_sem=w_recv.at[slot],
            device_id={"dp": to},
        )

    for turn in range(pieces):
        piece = piece_of(turn)
        last = turn == pieces - 1

        def take_grads(step, carry):
            source = origin(step)
            grads_copy(piece, source, source, source).wait_recv()
            done = back_part(piece, source)
            if turn > 0:
                done = done + back[source]
            if last:
                give_back(source, sent_back, done)
                back_copy(source, source, me).start()
            else:
                back[source] = done
            if turn + 2 < pieces:
                send_grads(turn + 2, step)
            return carry

        lax.fori_loop(0, experts - 1, take_grads, 0)
        mine = back_part(piece, me)
        if turn > 0:
            mine = mine + back[me]
        if last:
            give_back(me, got_back, mine)
        else:
            back[me] = mine
        down = lax.dot_general(
            act[...].reshape(experts * slots, act.shape[2]),
            got_grads[piece].reshape(experts * slots, width),
            BY_ROWS,
            preferred_element_type=jnp.float32,
        ).astype(jnp.bfloat16)
        for u in range(per_piece):
            to = piece * per_piece + u
            w_sent[to] = down[:, u * columns : (u + 1) * columns]
            if not last:
                share(to, group).start()
            elif per_piece > 1:
                pl.when(to != group)(lambda: share(to, group).start())

    def combine(source):
        pick = jnp.where(choose(source), 1.0, 0.0).astype(jnp.bfloat16)
        return lax.dot_general(pick, got_back[source], BY_ROWS, preferred_element_type=jnp.float32)

    total[...] = combine(me)

    w_own[...] = w_sent[group].astype(jnp.float32)

    def gather(step, carry):
        source = (group + step) % groups
        share(source, source).wait_recv()
        w_own[...] += w_got[source].astype(jnp.float32)
        return carry

    lax.fori_loop(1, groups, gather, 0)
    grad_w[...] = w_own[...].astype(jnp.bfloat16)

    def take_back(step, carry):
        source = target(step)
        back_copy(source, source, source).wait_recv()
        total[...] += combine(source)
        return carry

    lax.fori_loop(0, experts - 1, take_back, 0)
    grad_tokens[...] = total[...].astype(jnp.bfloat16)

    def drain(step, carry):
        to = target(step)
        rows_copy(to, to, me).wait_send()
        for p in range(pieces):
            grads_copy(p, to, to, me).wait_send()
        back_copy(to, to, me).wait_send()
        return carry

    def drain_group(step, carry):
        share((group + step) % groups, group).wait_send()
        return carry

    lax.fori_loop(0, experts - 1, drain, 0)
    lax.fori_loop(1, groups, drain_group, 0)


def hand_over(first, second, first_out, second_out, sems):
    copies = [
        pltpu.make_async_copy(first, first_out, sems.at[0]),
        pltpu.make_async_copy(second, second_out, sems.at[1]),
    ]
    for copy in copies:
        copy.start()
    for copy in copies:
        copy.wait()


def per_device(tokens, cotangent, gates, expert_ids, w_in, w_out):
    rows, width = tokens.shape
    hidden = w_out.shape[1]
    experts, groups = lax.axis_size("expert"), lax.axis_size("dp")
    capacity = 5 * rows * expert_ids.shape[1] // (4 * experts)
    slots = -(-capacity // 8) * 8
    columns = width // groups
    pieces = 4 if groups % 4 == 0 else 1
    blocks = pltpu.VMEM((experts, slots, width), jnp.bfloat16)
    parts = pltpu.VMEM((pieces, experts, slots, width // pieces), jnp.bfloat16)
    shares = pltpu.VMEM((groups, hidden, columns), jnp.bfloat16)
    vmem = pl.BlockSpec(memory_space=pltpu.VMEM)
    anywhere = pl.BlockSpec(memory_space=pl.ANY)
    multiplies = experts * slots * width * hidden
    outs = (
        jax.ShapeDtypeStruct((rows, width), jnp.bfloat16),
        jax.ShapeDtypeStruct((hidden, columns), jnp.bfloat16),
    )
    results = pl.pallas_call(
        functools.partial(layer_kernel, experts, groups, pieces),
        out_shape=outs,
        in_specs=[vmem] * 4 + [anywhere] * 2,
        out_specs=(vmem, vmem),
        scratch_shapes=[
            pltpu.VMEM((hidden, width), jnp.bfloat16),
            pltpu.VMEM((pieces, hidden, width // pieces), jnp.bfloat16),
            pltpu.VMEM((experts, rows), jnp.float32),
            pltpu.VMEM((experts, rows), jnp.float32),
            blocks,
            parts,
            blocks,
            parts,
            pltpu.VMEM((experts, slots, hidden), jnp.bfloat16),
            pltpu.VMEM((experts, slots, hidden), jnp.float32),
            pltpu.VMEM((experts, slots, hidden), jnp.float32),
            blocks,
            blocks,
            pltpu.VMEM((rows, width), jnp.float32),
            pltpu.VMEM((hidden, columns), jnp.float32),
            shares,
            shares,
            pltpu.SemaphoreType.DMA((pieces + 1,)),
            pltpu.SemaphoreType.DMA((experts,)),
            pltpu.SemaphoreType.DMA((experts,)),
            pltpu.SemaphoreType.DMA((pieces, experts)),
            pltpu.SemaphoreType.DMA((pieces, experts)),
            pltpu.SemaphoreType.DMA((experts,)),
            pltpu.SemaphoreType.DMA((experts,)),
            pltpu.SemaphoreType.DMA((groups,)),
            pltpu.SemaphoreType.DMA((groups,)),
        ],
        compiler_params=pltpu.CompilerParams(
            collective_id=0, has_side_effects=True, vmem_limit_bytes=56 * 1024 * 1024
        ),
        cost_estimate=pl.CostEstimate(
            flops=8 * multiplies, bytes_accessed=4 * hidden * width, transcendentals=0
        ),
    )(
        tokens,
        cotangent,
        gates.T,
        expert_ids.T,
        jnp.swapaxes(w_in[0], 0, 1),
        w_out[0],
    )
    grad_tokens, grad_w = pl.pallas_call(
        hand_over,
        out_shape=outs,
        in_specs=[anywhere] * 2,
        out_specs=(anywhere, anywhere),
        scratch_shapes=[pltpu.SemaphoreType.DMA((2,))],
        compiler_params=pltpu.CompilerParams(vmem_limit_bytes=56 * 1024 * 1024),
    )(*results)
    return grad_tokens, grad_w[None]


def solution(mesh):
    split = P(("expert", "dp"), None)
    whole = P("expert", None, None)
    return jax.shard_map(
        per_device,
        mesh=mesh,
        in_specs=(split, split, split, split, whole, whole),
        out_specs=(split, P("expert", None, "dp")),
        check_vma=False,
    )
```

```python
import functools

import jax
import jax.numpy as jnp
from jax import lax
from jax.experimental import pallas as pl
from jax.experimental.pallas import tpu as pltpu
from jax.sharding import PartitionSpec as P

BY_COLS = (((1,), (1,)), ((), ()))
BY_ROWS = (((0,), (0,)), ((), ()))


def layer_kernel(
    experts, groups, pieces, tokens, cotangent, gates, ids, w_in_hbm, w_out_hbm, grad_tokens,
    grad_w, w_in, w_out, places, gains, sent_rows, sent_grads, got_rows, got_grads, act, slope,
    back, sent_back, got_back, total, w_own, w_sent, w_got, load_sems, row_send, row_recv,
    grad_send, grad_recv, back_send, back_recv, w_send, w_recv,
):
    me = lax.axis_index("expert")
    group = lax.axis_index("dp")
    half = experts // 2
    slots = got_rows.shape[1]
    columns = grad_w.shape[1]
    per_piece = groups // pieces
    width = per_piece * columns
    my_piece = group // per_piece

    loads = [pltpu.make_async_copy(w_in_hbm, w_in, load_sems.at[pieces])] + [
        pltpu.make_async_copy(
            w_out_hbm.at[:, pl.ds(p * width, width)], w_out.at[p], load_sems.at[p]
        )
        for p in range(pieces)
    ]
    for load in loads:
        load.start()

    barrier = pltpu.get_barrier_semaphore()

    def greet_expert(step, carry):
        pl.semaphore_signal(barrier, inc=1, device_id={"expert": (me + step) % experts})
        return carry

    def greet_group(step, carry):
        pl.semaphore_signal(barrier, inc=1, device_id={"dp": (group + step) % groups})
        return carry

    lax.fori_loop(1, experts, greet_expert, 0)
    lax.fori_loop(1, groups, greet_group, 0)

    my_half = me // half
    other = (1 - my_half) * half

    def target(step):
        return jnp.where(
            step < half, other + (me + step) % half, my_half * half + (me + step - half + 1) % half
        )

    def origin(step):
        return jnp.where(
            step < half,
            other + (me + half - step % half) % half,
            my_half * half + (me + 2 * half - step % half - 1) % half,
        )

    def piece_of(turn):
        return (my_piece + 1 + turn) % pieces

    def rows_copy(to, here, there):
        return pltpu.make_async_remote_copy(
            src_ref=sent_rows.at[here],
            dst_ref=got_rows.at[there],
            send_sem=row_send.at[here],
            recv_sem=row_recv.at[there],
            device_id={"expert": to},
        )

    def grads_copy(piece, to, here, there):
        return pltpu.make_async_remote_copy(
            src_ref=sent_grads.at[piece, here],
            dst_ref=got_grads.at[piece, there],
            send_sem=grad_send.at[piece, here],
            recv_sem=grad_recv.at[piece, there],
            device_id={"expert": to},
        )

    def back_copy(to, here, there):
        return pltpu.make_async_remote_copy(
            src_ref=sent_back.at[here],
            dst_ref=got_back.at[there],
            send_sem=back_send.at[here],
            recv_sem=back_recv.at[there],
            device_id={"expert": to},
        )

    rows = tokens.shape[0]
    expert_of = lax.broadcasted_iota(jnp.int32, (experts, rows), 0)
    chosen = jnp.zeros((experts, rows), jnp.float32)
    gain = jnp.zeros((experts, rows), jnp.float32)
    for k in range(ids.shape[0]):
        hit = expert_of == ids[k : k + 1, :]
        chosen = chosen + jnp.where(hit, 1.0, 0.0)
        gain = gain + jnp.where(hit, gates[k : k + 1, :], 0.0)
    earlier = jnp.where(
        lax.broadcasted_iota(jnp.int32, (rows, rows), 0)
        < lax.broadcasted_iota(jnp.int32, (rows, rows), 1),
        1.0,
        0.0,
    ).astype(jnp.bfloat16)
    place = jnp.dot(chosen.astype(jnp.bfloat16), earlier, preferred_element_type=jnp.float32)
    places[...] = jnp.where(chosen > 0.0, place, -1.0)
    gains[...] = gain
    slot_number = lax.broadcasted_iota(jnp.int32, (slots, rows), 0).astype(jnp.float32)

    def choose(expert):
        return slot_number == places[pl.ds(expert, 1), :]

    def pack_rows(expert, into):
        pick = jnp.where(choose(expert), 1.0, 0.0).astype(jnp.bfloat16)
        picked = jnp.dot(pick, tokens[...], preferred_element_type=jnp.float32)
        into[expert] = picked.astype(jnp.bfloat16)

    def pack_grads(piece, expert, into):
        match = choose(expert)
        pick = jnp.where(match, 1.0, 0.0).astype(jnp.bfloat16)
        weight = jnp.sum(jnp.where(match, gains[pl.ds(expert, 1), :], 0.0), axis=1, keepdims=True)
        part = cotangent[:, pl.ds(pl.multiple_of(piece * width, width), width)]
        gated = jnp.dot(pick, part, preferred_element_type=jnp.float32) * weight
        into[piece, expert] = gated.astype(jnp.bfloat16)

    pl.semaphore_wait(barrier, experts + groups - 2)

    def send_rows(step, carry):
        to = target(step)
        pack_rows(to, sent_rows)
        rows_copy(to, to, me).start()
        return carry

    def send_grads(turn, step):
        to = target(step)
        piece = piece_of(turn)
        pack_grads(piece, to, sent_grads)
        grads_copy(piece, to, to, me).start()

    def send_first_grads(step, carry):
        send_grads(0, step)
        return carry

    lax.fori_loop(0, experts - 1, send_rows, 0)
    lax.fori_loop(0, experts - 1, send_first_grads, 0)
    pack_rows(me, got_rows)
    for p in range(pieces):
        pack_grads(p, me, got_grads)
    for load in loads:
        load.wait()

    def absorb_rows(source):
        pre = lax.dot_general(
            got_rows[source], w_in[...], BY_COLS, preferred_element_type=jnp.float32
        )
        sig = 1.0 / (1.0 + jnp.exp(-pre))
        act[source] = (pre * sig).astype(jnp.bfloat16)
        slope[source] = sig * (1.0 + pre * (1.0 - sig))

    def take_rows(step, carry):
        source = origin(step)
        rows_copy(source, source, source).wait_recv()
        absorb_rows(source)
        if pieces > 1:
            send_grads(1, step)
        return carry

    absorb_rows(me)
    lax.fori_loop(0, experts - 1, take_rows, 0)

    def back_part(piece, source):
        return lax.dot_general(
            got_grads[piece, source], w_out[piece], BY_COLS, preferred_element_type=jnp.float32
        )

    def give_back(source, into, done):
        dpre = (done * slope[source]).astype(jnp.bfloat16)
        into[source] = jnp.dot(dpre, w_in[...], preferred_element_type=jnp.float32).astype(
            jnp.bfloat16
        )

    def share(to, slot):
        return pltpu.make_async_remote_copy(
            src_ref=w_sent.at[to],
            dst_ref=w_got.at[slot],
            send_sem=w_send.at[to],
            recv_sem=w_recv.at[slot],
            device_id={"dp": to},
        )

    for turn in range(pieces):
        piece = piece_of(turn)
        last = turn == pieces - 1

        def take_grads(step, carry):
            source = origin(step)
            grads_copy(piece, source, source, source).wait_recv()
            done = back_part(piece, source)
            if turn > 0:
                done = done + back[source]
            if last:
                give_back(source, sent_back, done)
                back_copy(source, source, me).start()
            else:
                back[source] = done
            if turn + 2 < pieces:
                send_grads(turn + 2, step)
            return carry

        lax.fori_loop(0, experts - 1, take_grads, 0)
        mine = back_part(piece, me)
        if turn > 0:
            mine = mine + back[me]
        if last:
            give_back(me, got_back, mine)
        else:
            back[me] = mine
        down = lax.dot_general(
            act[...].reshape(experts * slots, act.shape[2]),
            got_grads[piece].reshape(experts * slots, width),
            BY_ROWS,
            preferred_element_type=jnp.float32,
        ).astype(jnp.bfloat16)
        for u in range(per_piece):
            to = piece * per_piece + u
            w_sent[to] = down[:, u * columns : (u + 1) * columns]
            if not last:
                share(to, group).start()
            elif per_piece > 1:
                pl.when(to != group)(lambda: share(to, group).start())

    def combine(source):
        pick = jnp.where(choose(source), 1.0, 0.0).astype(jnp.bfloat16)
        return lax.dot_general(pick, got_back[source], BY_ROWS, preferred_element_type=jnp.float32)

    total[...] = combine(me)

    w_own[...] = w_sent[group].astype(jnp.float32)

    def gather(step, carry):
        source = (group + step) % groups
        share(source, source).wait_recv()
        w_own[...] += w_got[source].astype(jnp.float32)
        return carry

    lax.fori_loop(1, groups, gather, 0)
    grad_w[...] = w_own[...].astype(jnp.bfloat16)

    def take_back(step, carry):
        source = target(step)
        back_copy(source, source, source).wait_recv()
        total[...] += combine(source)
        return carry

    lax.fori_loop(0, experts - 1, take_back, 0)
    grad_tokens[...] = total[...].astype(jnp.bfloat16)

    def drain(step, carry):
        to = target(step)
        rows_copy(to, to, me).wait_send()
        for p in range(pieces):
            grads_copy(p, to, to, me).wait_send()
        back_copy(to, to, me).wait_send()
        return carry

    def drain_group(step, carry):
        share((group + step) % groups, group).wait_send()
        return carry

    lax.fori_loop(0, experts - 1, drain, 0)
    lax.fori_loop(1, groups, drain_group, 0)


def hand_over(first, second, first_out, second_out, first_held, second_held, sems):
    steps = []
    for ref, held, out, which in (
        (first, first_held, first_out, 0),
        (second, second_held, second_out, 1),
    ):
        steps.append(
            (
                pltpu.make_async_copy(ref, held, sems.at[0, which]),
                pltpu.make_async_copy(held, out, sems.at[1, which]),
            )
        )
    for load, _ in steps:
        load.start()
    for load, store in steps:
        load.wait()
        store.start()
    for _, store in steps:
        store.wait()


def per_device(tokens, cotangent, gates, expert_ids, w_in, w_out):
    rows, width = tokens.shape
    hidden = w_out.shape[1]
    experts, groups = lax.axis_size("expert"), lax.axis_size("dp")
    capacity = 5 * rows * expert_ids.shape[1] // (4 * experts)
    slots = -(-capacity // 8) * 8
    columns = width // groups
    pieces = 4 if groups % 4 == 0 else 1
    blocks = pltpu.VMEM((experts, slots, width), jnp.bfloat16)
    parts = pltpu.VMEM((pieces, experts, slots, width // pieces), jnp.bfloat16)
    shares = pltpu.VMEM((groups, hidden, columns), jnp.bfloat16)
    vmem = pl.BlockSpec(memory_space=pltpu.VMEM)
    anywhere = pl.BlockSpec(memory_space=pl.ANY)
    multiplies = experts * slots * width * hidden
    outs = (
        jax.ShapeDtypeStruct((rows, width), jnp.bfloat16),
        jax.ShapeDtypeStruct((hidden, columns), jnp.bfloat16),
    )
    results = pl.pallas_call(
        functools.partial(layer_kernel, experts, groups, pieces),
        out_shape=outs,
        in_specs=[vmem] * 4 + [anywhere] * 2,
        out_specs=(vmem, vmem),
        scratch_shapes=[
            pltpu.VMEM((hidden, width), jnp.bfloat16),
            pltpu.VMEM((pieces, hidden, width // pieces), jnp.bfloat16),
            pltpu.VMEM((experts, rows), jnp.float32),
            pltpu.VMEM((experts, rows), jnp.float32),
            blocks,
            parts,
            blocks,
            parts,
            pltpu.VMEM((experts, slots, hidden), jnp.bfloat16),
            pltpu.VMEM((experts, slots, hidden), jnp.float32),
            pltpu.VMEM((experts, slots, hidden), jnp.float32),
            blocks,
            blocks,
            pltpu.VMEM((rows, width), jnp.float32),
            pltpu.VMEM((hidden, columns), jnp.float32),
            shares,
            shares,
            pltpu.SemaphoreType.DMA((pieces + 1,)),
            pltpu.SemaphoreType.DMA((experts,)),
            pltpu.SemaphoreType.DMA((experts,)),
            pltpu.SemaphoreType.DMA((pieces, experts)),
            pltpu.SemaphoreType.DMA((pieces, experts)),
            pltpu.SemaphoreType.DMA((experts,)),
            pltpu.SemaphoreType.DMA((experts,)),
            pltpu.SemaphoreType.DMA((groups,)),
            pltpu.SemaphoreType.DMA((groups,)),
        ],
        compiler_params=pltpu.CompilerParams(
            collective_id=0, has_side_effects=True, vmem_limit_bytes=56 * 1024 * 1024
        ),
        cost_estimate=pl.CostEstimate(
            flops=8 * multiplies, bytes_accessed=4 * hidden * width, transcendentals=0
        ),
    )(
        tokens,
        cotangent,
        gates.T,
        expert_ids.T,
        jnp.swapaxes(w_in[0], 0, 1),
        w_out[0],
    )
    grad_tokens, grad_w = pl.pallas_call(
        hand_over,
        out_shape=outs,
        in_specs=[anywhere] * 2,
        out_specs=(anywhere, anywhere),
        scratch_shapes=[
            pltpu.VMEM(outs[0].shape, jnp.bfloat16),
            pltpu.VMEM(outs[1].shape, jnp.bfloat16),
            pltpu.SemaphoreType.DMA((2, 2)),
        ],
        compiler_params=pltpu.CompilerParams(vmem_limit_bytes=56 * 1024 * 1024),
    )(*results)
    return grad_tokens, grad_w[None]


def solution(mesh):
    split = P(("expert", "dp"), None)
    whole = P("expert", None, None)
    return jax.shard_map(
        per_device,
        mesh=mesh,
        in_specs=(split, split, split, split, whole, whole),
        out_specs=(split, P("expert", None, "dp")),
        check_vma=False,
    )
```

```python
import functools

import jax
import jax.numpy as jnp
from jax import lax
from jax.experimental import pallas as pl
from jax.experimental.pallas import tpu as pltpu
from jax.sharding import PartitionSpec as P

BY_COLS = (((1,), (1,)), ((), ()))
BY_ROWS = (((0,), (0,)), ((), ()))


AHEAD = 3


def layer_kernel(
    experts, groups, pieces, tokens, cotangent, gates, ids, w_in_hbm, w_out_hbm, grad_tokens,
    grad_w, w_in, w_out, table, table_got, raw, sent, passed, got, sums, act, slope, dpre,
    sent_back, got_back, relay_back, relay_sum, far, total, w_own, w_sent, w_got, load_sems,
    table_sems, raw_send, raw_recv, sent_sems, passed_sems, got_sems, back_send, back_recv,
    relay_recv, sum_send, far_sems, w_send, w_recv,
):
    me = lax.axis_index("expert")
    group = lax.axis_index("dp")
    half = experts // 2
    relays = half // 2
    slots = got.shape[2]
    rows = tokens.shape[0]
    columns = grad_w.shape[1]
    per_piece = groups // pieces
    width = per_piece * columns
    turns = 2 * pieces
    my_piece = group // per_piece

    loads = [
        pltpu.make_async_copy(hbm.at[:, pl.ds(p * width, width)], held.at[p], load_sems.at[k, p])
        for k, (hbm, held) in enumerate(((w_in_hbm, w_in), (w_out_hbm, w_out)))
        for p in range(pieces)
    ]
    for load in loads:
        load.start()

    barrier = pltpu.get_barrier_semaphore()

    def greet_expert(step, carry):
        pl.semaphore_signal(barrier, inc=1, device_id={"expert": (me + step) % experts})
        return carry

    def greet_group(step, carry):
        pl.semaphore_signal(barrier, inc=1, device_id={"dp": (group + step) % groups})
        return carry

    lax.fori_loop(1, experts, greet_expert, 0)
    lax.fori_loop(1, groups, greet_group, 0)

    side = me // half
    spot = me % half
    home = side * half
    away = (1 - side) * half
    number = spot % relays
    is_relay = spot // relays == 1 - side
    my_relay = side * relays + (1 - side) * half + number
    home_relays = (1 - side) * relays + side * half

    def peer_of(step):
        return home + (spot + step) % half

    def away_of(u):
        return away + number + u * relays

    def piece_of(turn):
        return (my_piece + 1 + turn) % pieces

    def index_of(turn):
        return (turn // pieces) * pieces + piece_of(turn % pieces)

    def remote(source, dest, send_sem, recv_sem, to):
        return pltpu.make_async_remote_copy(
            src_ref=source,
            dst_ref=dest,
            send_sem=send_sem,
            recv_sem=recv_sem,
            device_id={"expert": to},
        )

    def table_copy(slot, to):
        return remote(table, table_got.at[slot], table_sems.at[2], table_sems.at[slot], to)

    def raw_copy(turn, slot, to):
        part = tokens if turn < pieces else cotangent
        start = pl.multiple_of(piece_of(turn % pieces) * width, width)
        index = index_of(turn)
        return remote(
            part.at[:, pl.ds(start, width)],
            raw.at[slot, index],
            raw_send.at[index],
            raw_recv.at[slot, index],
            to,
        )

    def sent_copy(index, step, slot, to):
        return remote(
            sent.at[index, step],
            got.at[index, slot],
            sent_sems.at[index, step],
            got_sems.at[index, slot],
            to,
        )

    def passed_copy(index, u, step, slot, to):
        return remote(
            passed.at[index, u, step],
            got.at[index, slot],
            passed_sems.at[index, u, step],
            got_sems.at[index, slot],
            to,
        )

    expert_of = lax.broadcasted_iota(jnp.int32, (experts, rows), 0)
    chosen = jnp.zeros((experts, rows), jnp.float32)
    gain = jnp.zeros((experts, rows), jnp.float32)
    for k in range(ids.shape[0]):
        hit = expert_of == ids[k : k + 1, :]
        chosen = chosen + jnp.where(hit, 1.0, 0.0)
        gain = gain + jnp.where(hit, gates[k : k + 1, :], 0.0)
    earlier = jnp.where(
        lax.broadcasted_iota(jnp.int32, (rows, rows), 0)
        < lax.broadcasted_iota(jnp.int32, (rows, rows), 1),
        1.0,
        0.0,
    ).astype(jnp.bfloat16)
    place = jnp.dot(chosen.astype(jnp.bfloat16), earlier, preferred_element_type=jnp.float32)
    table[0] = jnp.where(chosen > 0.0, place, -1.0)
    table[1] = gain
    slot_number = lax.broadcasted_iota(jnp.int32, (slots, rows), 0).astype(jnp.float32)

    def pack(turn, held, expert, part):
        match = slot_number == held[0, pl.ds(expert, 1), :]
        pick = jnp.where(match, 1.0, 0.0).astype(jnp.bfloat16)
        out = jnp.dot(pick, part, preferred_element_type=jnp.float32)
        if turn >= pieces:
            gain_row = held[1, pl.ds(expert, 1), :]
            out = out * jnp.sum(jnp.where(match, gain_row, 0.0), axis=1, keepdims=True)
        return out.astype(jnp.bfloat16)

    def own_part(turn):
        part = tokens if turn < pieces else cotangent
        return part[:, pl.ds(pl.multiple_of(piece_of(turn % pieces) * width, width), width)]

    pl.semaphore_wait(barrier, experts + groups - 2)

    def send(turn):
        index = index_of(turn)
        raw_copy(turn, spot // relays, my_relay).start()

        def to_peer(step, carry):
            to = peer_of(step)
            sent[index, step] = pack(turn, table, to, own_part(turn))
            sent_copy(index, step, me, to).start()
            return carry

        lax.fori_loop(1, half, to_peer, 0)
        got[index, me] = pack(turn, table, me, own_part(turn))

    table_copy(spot // relays, my_relay).start()
    for turn in range(AHEAD):
        send(turn)
    for load in loads:
        load.wait()

    def pass_on(turn):
        index = index_of(turn)
        for u in range(2):
            source = away_of(u)
            if turn == 0:
                table_copy(u, source).wait_recv()
            raw_copy(turn, u, source).wait_recv()

            def to_peer(step, carry):
                to = peer_of(step)
                passed[index, u, step] = pack(turn, table_got.at[u], to, raw[u, index])
                passed_copy(index, u, step, source, to).start()
                return carry

            lax.fori_loop(1, half, to_peer, 0)
            got[index, source] = pack(turn, table_got.at[u], me, raw[u, index])

    def receive(turn):
        index = index_of(turn)

        def from_peer(step, carry):
            source = peer_of(step)
            sent_copy(index, step, source, source).wait_recv()
            return carry

        def from_away(step, carry):
            source = away + step

            def wait():
                passed_copy(index, 0, 0, source, source).wait_recv()

            pl.when(home_relays + step % relays != me)(wait)
            return carry

        lax.fori_loop(1, half, from_peer, 0)
        lax.fori_loop(0, half, from_away, 0)

    def share(to, slot):
        return pltpu.make_async_remote_copy(
            src_ref=w_sent.at[to],
            dst_ref=w_got.at[slot],
            send_sem=w_send.at[to],
            recv_sem=w_recv.at[slot],
            device_id={"dp": to},
        )

    flat = experts * slots
    hidden = act.shape[1]

    def down_part(turn):
        piece = piece_of(turn % pieces)
        down = lax.dot_general(
            act[...],
            got[index_of(turn)].reshape(flat, width),
            BY_ROWS,
            preferred_element_type=jnp.float32,
        ).astype(jnp.bfloat16)
        last = turn == turns - 1
        for u in range(per_piece):
            to = piece * per_piece + u
            w_sent[to] = down[:, u * columns : (u + 1) * columns]
            if not last:
                share(to, group).start()
            elif per_piece > 1:
                pl.when(to != group)(lambda: share(to, group).start())

    for turn in range(turns):
        pl.when(is_relay)(functools.partial(pass_on, turn))
        if turn + AHEAD < turns:
            send(turn + AHEAD)
        receive(turn)
        weights = w_in if turn < pieces else w_out
        part = lax.dot_general(
            got[index_of(turn)].reshape(flat, width),
            weights[piece_of(turn % pieces)],
            BY_COLS,
            preferred_element_type=jnp.float32,
        )
        if turn % pieces > 0:
            part = part + sums[...]
        if turn == pieces - 1:
            sig = 1.0 / (1.0 + jnp.exp(-part))
            act[...] = (part * sig).astype(jnp.bfloat16)
            slope[...] = sig * (1.0 + part * (1.0 - sig))
        elif turn == turns - 1:
            dpre[...] = (part * slope[...]).astype(jnp.bfloat16).reshape(experts, slots, hidden)
        else:
            sums[...] = part
        if pieces <= turn < turns - 1:
            down_part(turn)

    def give_back(source, into):
        for p in range(pieces):
            into[:, p * width : (p + 1) * width] = jnp.dot(
                dpre[source], w_in[p], preferred_element_type=jnp.float32
            ).astype(jnp.bfloat16)

    def relay_copy(source, slot, at, to):
        return remote(
            sent_back.at[source],
            relay_back.at[slot, at],
            back_send.at[source],
            relay_recv.at[slot, at],
            to,
        )

    def back_copy(to, slot):
        return remote(
            sent_back.at[to], got_back.at[slot], back_send.at[to], back_recv.at[slot], to
        )

    def back_away(step, carry):
        source = away + step
        relay = home_relays + step % relays
        slot = step // relays

        def keep():
            give_back(source, relay_back.at[slot, spot])

        def hand():
            give_back(source, sent_back.at[source])
            relay_copy(source, slot, spot, relay).start()

        pl.when(relay == me)(keep)
        pl.when(relay != me)(hand)
        return carry

    lax.fori_loop(0, half, back_away, 0)

    def combine(held, expert, block):
        match = slot_number == held[0, pl.ds(expert, 1), :]
        pick = jnp.where(match, 1.0, 0.0).astype(jnp.bfloat16)
        return lax.dot_general(pick, block, BY_ROWS, preferred_element_type=jnp.float32)

    def far_copy(u, to):
        return remote(relay_sum.at[u], far, sum_send.at[u], far_sems.at[0], to)

    def relay_sums():
        for u in range(2):
            total[...] = combine(table_got.at[u], me, relay_back[u, spot])

            def add(step, carry):
                peer = peer_of(step)
                at = (spot + step) % half
                relay_copy(me, u, at, peer).wait_recv()
                total[...] += combine(table_got.at[u], peer, relay_back[u, at])
                return carry

            lax.fori_loop(1, half, add, 0)
            relay_sum[u] = total[...].astype(jnp.bfloat16)
            far_copy(u, away_of(u)).start()

    pl.when(is_relay)(relay_sums)

    def back_home(step, carry):
        to = peer_of(step)
        give_back(to, sent_back.at[to])
        back_copy(to, me).start()
        return carry

    lax.fori_loop(1, half, back_home, 0)
    give_back(me, got_back.at[me])
    down_part(turns - 1)
    total[...] = combine(table, me, got_back[me])

    w_own[...] = w_sent[group].astype(jnp.float32)

    def gather(step, carry):
        source = (group + step) % groups
        share(source, source).wait_recv()
        w_own[...] += w_got[source].astype(jnp.float32)
        return carry

    lax.fori_loop(1, groups, gather, 0)
    grad_w[...] = w_own[...].astype(jnp.bfloat16)

    def take_back(step, carry):
        source = peer_of(step)
        back_copy(source, source).wait_recv()
        total[...] += combine(table, source, got_back[source])
        return carry

    lax.fori_loop(1, half, take_back, 0)
    far_copy(0, my_relay).wait_recv()
    grad_tokens[...] = (total[...] + far[...].astype(jnp.float32)).astype(jnp.bfloat16)

    table_copy(0, my_relay).wait_send()
    for turn in range(turns):
        index = index_of(turn)
        raw_copy(turn, 0, my_relay).wait_send()

        def drain_sent(step, carry):
            sent_copy(index, step, me, peer_of(step)).wait_send()
            return carry

        def drain_passed(step, carry):
            for u in range(2):
                passed_copy(index, u, step, me, peer_of(step)).wait_send()
            return carry

        lax.fori_loop(1, half, drain_sent, 0)

        def drain_all_passed():
            lax.fori_loop(1, half, drain_passed, 0)

        pl.when(is_relay)(drain_all_passed)

    def drain_away(step, carry):
        relay = home_relays + step % relays

        def wait():
            relay_copy(away + step, 0, 0, relay).wait_send()

        pl.when(relay != me)(wait)
        return carry

    def drain_home(step, carry):
        back_copy(peer_of(step), me).wait_send()
        return carry

    def drain_sums():
        for u in range(2):
            far_copy(u, away_of(u)).wait_send()

    def drain_group(step, carry):
        share((group + step) % groups, group).wait_send()
        return carry

    lax.fori_loop(0, half, drain_away, 0)
    lax.fori_loop(1, half, drain_home, 0)
    pl.when(is_relay)(drain_sums)
    lax.fori_loop(1, groups, drain_group, 0)


def hand_over(first, second, first_out, second_out, first_held, second_held, sems):
    steps = []
    for ref, held, out, which in (
        (first, first_held, first_out, 0),
        (second, second_held, second_out, 1),
    ):
        steps.append(
            (
                pltpu.make_async_copy(ref, held, sems.at[0, which]),
                pltpu.make_async_copy(held, out, sems.at[1, which]),
            )
        )
    for load, _ in steps:
        load.start()
    for load, store in steps:
        load.wait()
        store.start()
    for _, store in steps:
        store.wait()


def per_device(tokens, cotangent, gates, expert_ids, w_in, w_out):
    rows, width = tokens.shape
    hidden = w_out.shape[1]
    experts, groups = lax.axis_size("expert"), lax.axis_size("dp")
    capacity = 5 * rows * expert_ids.shape[1] // (4 * experts)
    slots = -(-capacity // 8) * 8
    columns = width // groups
    pieces = 4 if groups % 4 == 0 else 1
    half, turns, part = experts // 2, 2 * pieces, width // pieces
    shares = pltpu.VMEM((groups, hidden, columns), jnp.bfloat16)
    vmem = pl.BlockSpec(memory_space=pltpu.VMEM)
    anywhere = pl.BlockSpec(memory_space=pl.ANY)
    multiplies = experts * slots * width * hidden
    outs = (
        jax.ShapeDtypeStruct((rows, width), jnp.bfloat16),
        jax.ShapeDtypeStruct((hidden, columns), jnp.bfloat16),
    )
    results = pl.pallas_call(
        functools.partial(layer_kernel, experts, groups, pieces),
        out_shape=outs,
        in_specs=[vmem] * 4 + [anywhere] * 2,
        out_specs=(vmem, vmem),
        scratch_shapes=[
            pltpu.VMEM((pieces, hidden, part), jnp.bfloat16),
            pltpu.VMEM((pieces, hidden, part), jnp.bfloat16),
            pltpu.VMEM((2, experts, rows), jnp.float32),
            pltpu.VMEM((2, 2, experts, rows), jnp.float32),
            pltpu.VMEM((2, turns, rows, part), jnp.bfloat16),
            pltpu.VMEM((turns, half, slots, part), jnp.bfloat16),
            pltpu.VMEM((turns, 2, half, slots, part), jnp.bfloat16),
            pltpu.VMEM((turns, experts, slots, part), jnp.bfloat16),
            pltpu.VMEM((experts * slots, hidden), jnp.float32),
            pltpu.VMEM((experts * slots, hidden), jnp.bfloat16),
            pltpu.VMEM((experts * slots, hidden), jnp.float32),
            pltpu.VMEM((experts, slots, hidden), jnp.bfloat16),
            pltpu.VMEM((experts, slots, width), jnp.bfloat16),
            pltpu.VMEM((experts, slots, width), jnp.bfloat16),
            pltpu.VMEM((2, half, slots, width), jnp.bfloat16),
            pltpu.VMEM((2, rows, width), jnp.bfloat16),
            pltpu.VMEM((rows, width), jnp.bfloat16),
            pltpu.VMEM((rows, width), jnp.float32),
            pltpu.VMEM((hidden, columns), jnp.float32),
            shares,
            shares,
            pltpu.SemaphoreType.DMA((2, pieces)),
            pltpu.SemaphoreType.DMA((3,)),
            pltpu.SemaphoreType.DMA((turns,)),
            pltpu.SemaphoreType.DMA((2, turns)),
            pltpu.SemaphoreType.DMA((turns, half)),
            pltpu.SemaphoreType.DMA((turns, 2, half)),
            pltpu.SemaphoreType.DMA((turns, experts)),
            pltpu.SemaphoreType.DMA((experts,)),
            pltpu.SemaphoreType.DMA((experts,)),
            pltpu.SemaphoreType.DMA((2, half)),
            pltpu.SemaphoreType.DMA((2,)),
            pltpu.SemaphoreType.DMA((1,)),
            pltpu.SemaphoreType.DMA((groups,)),
            pltpu.SemaphoreType.DMA((groups,)),
        ],
        compiler_params=pltpu.CompilerParams(
            collective_id=0, has_side_effects=True, vmem_limit_bytes=56 * 1024 * 1024
        ),
        cost_estimate=pl.CostEstimate(
            flops=8 * multiplies, bytes_accessed=4 * hidden * width, transcendentals=0
        ),
    )(
        tokens,
        cotangent,
        gates.T,
        expert_ids.T,
        jnp.swapaxes(w_in[0], 0, 1),
        w_out[0],
    )
    grad_tokens, grad_w = pl.pallas_call(
        hand_over,
        out_shape=outs,
        in_specs=[anywhere] * 2,
        out_specs=(anywhere, anywhere),
        scratch_shapes=[
            pltpu.VMEM(outs[0].shape, jnp.bfloat16),
            pltpu.VMEM(outs[1].shape, jnp.bfloat16),
            pltpu.SemaphoreType.DMA((2, 2)),
        ],
        compiler_params=pltpu.CompilerParams(vmem_limit_bytes=56 * 1024 * 1024),
    )(*results)
    return grad_tokens, grad_w[None]


def solution(mesh):
    split = P(("expert", "dp"), None)
    whole = P("expert", None, None)
    return jax.shard_map(
        per_device,
        mesh=mesh,
        in_specs=(split, split, split, split, whole, whole),
        out_specs=(split, P("expert", None, "dp")),
        check_vma=False,
    )
```

```python
import functools

import jax
import jax.numpy as jnp
from jax import lax
from jax.experimental import pallas as pl
from jax.experimental.pallas import tpu as pltpu
from jax.sharding import PartitionSpec as P

BY_COLS = (((1,), (1,)), ((), ()))
BY_ROWS = (((0,), (0,)), ((), ()))


AHEAD = 3


def layer_kernel(
    experts, groups, pieces, tokens, cotangent, gates, ids, w_in_hbm, w_out_hbm, grad_tokens,
    grad_w, w_in, w_out, table, table_got, picks, weights_of, raw, sent, passed, got, sums,
    act, slope, dpre, sent_home, sent_away, got_back, relay_back, relay_sum, far, w_own, w_sent, w_got, load_sems,
    table_sems, raw_send, raw_recv, sent_sems, passed_sems, got_sems, home_send, away_send,
    back_recv, relay_recv, sum_send, far_recv, w_send, w_recv,
):
    me = lax.axis_index("expert")
    group = lax.axis_index("dp")
    half = experts // 2
    relays = half // 2
    slots = got.shape[2]
    rows = tokens.shape[0]
    columns = grad_w.shape[1]
    per_piece = groups // pieces
    width = per_piece * columns
    turns = 2 * pieces
    my_piece = group // per_piece

    loads = [
        pltpu.make_async_copy(hbm.at[:, pl.ds(p * width, width)], held.at[p], load_sems.at[k, p])
        for k, (hbm, held) in enumerate(((w_in_hbm, w_in), (w_out_hbm, w_out)))
        for p in range(pieces)
    ]
    for load in loads:
        load.start()

    barrier = pltpu.get_barrier_semaphore()

    def greet_expert(step, carry):
        pl.semaphore_signal(barrier, inc=1, device_id={"expert": (me + step) % experts})
        return carry

    def greet_group(step, carry):
        pl.semaphore_signal(barrier, inc=1, device_id={"dp": (group + step) % groups})
        return carry

    lax.fori_loop(1, experts, greet_expert, 0)
    lax.fori_loop(1, groups, greet_group, 0)

    side = me // half
    spot = me % half
    home = side * half
    away = (1 - side) * half
    number = spot % relays
    is_relay = spot // relays == 1 - side
    my_relay = side * relays + (1 - side) * half + number
    home_relays = (1 - side) * relays + side * half

    def peer_of(step):
        return home + (spot + step) % half

    def away_of(u):
        return away + number + u * relays

    def piece_of(turn):
        return (my_piece + 1 + turn) % pieces

    def index_of(turn):
        return (turn // pieces) * pieces + piece_of(turn % pieces)

    def remote(source, dest, send_sem, recv_sem, to):
        return pltpu.make_async_remote_copy(
            src_ref=source,
            dst_ref=dest,
            send_sem=send_sem,
            recv_sem=recv_sem,
            device_id={"expert": to},
        )

    def table_copy(slot, to):
        return remote(table, table_got.at[slot], table_sems.at[2], table_sems.at[slot], to)

    def raw_copy(turn, slot, to):
        part = tokens if turn < pieces else cotangent
        start = pl.multiple_of(piece_of(turn % pieces) * width, width)
        index = index_of(turn)
        return remote(
            part.at[:, pl.ds(start, width)],
            raw.at[slot, index],
            raw_send.at[index],
            raw_recv.at[slot, index],
            to,
        )

    def sent_copy(index, step, slot, to):
        return remote(
            sent.at[index, step],
            got.at[index, slot],
            sent_sems.at[index, step],
            got_sems.at[index, slot],
            to,
        )

    def passed_copy(index, u, step, slot, to):
        return remote(
            passed.at[index, u, step],
            got.at[index, slot],
            passed_sems.at[index, u, step],
            got_sems.at[index, slot],
            to,
        )

    expert_of = lax.broadcasted_iota(jnp.int32, (experts, rows), 0)
    chosen = jnp.zeros((experts, rows), jnp.float32)
    gain = jnp.zeros((experts, rows), jnp.float32)
    for k in range(ids.shape[0]):
        hit = expert_of == ids[k : k + 1, :]
        chosen = chosen + jnp.where(hit, 1.0, 0.0)
        gain = gain + jnp.where(hit, gates[k : k + 1, :], 0.0)
    earlier = jnp.where(
        lax.broadcasted_iota(jnp.int32, (rows, rows), 0)
        < lax.broadcasted_iota(jnp.int32, (rows, rows), 1),
        1.0,
        0.0,
    ).astype(jnp.bfloat16)
    place = jnp.dot(chosen.astype(jnp.bfloat16), earlier, preferred_element_type=jnp.float32)
    table[0] = jnp.where(chosen > 0.0, place, -1.0)
    table[1] = gain
    slot_number = lax.broadcasted_iota(jnp.int32, (slots, rows), 0).astype(jnp.float32)

    def prepare(k, held):
        for step in range(half):
            expert = peer_of(step)
            match = slot_number == held[0, pl.ds(expert, 1), :]
            picks[k, step] = jnp.where(match, 1.0, 0.0).astype(jnp.bfloat16)
            gain_row = held[1, pl.ds(expert, 1), :]
            weights_of[k, step] = jnp.sum(
                jnp.where(match, gain_row, 0.0), axis=1, keepdims=True
            )

    def pick_of(k):
        return picks[k].reshape(half * slots, rows)

    def pack(turn, k, part):
        out = jnp.dot(pick_of(k), part, preferred_element_type=jnp.float32)
        if turn >= pieces:
            out = out * weights_of[k].reshape(half * slots, 1)
        return out.astype(jnp.bfloat16).reshape(half, slots, width)

    def own_part(turn):
        part = tokens if turn < pieces else cotangent
        return part[:, pl.ds(pl.multiple_of(piece_of(turn % pieces) * width, width), width)]

    pl.semaphore_wait(barrier, experts + groups - 2)

    def send(turn):
        index = index_of(turn)
        raw_copy(turn, spot // relays, my_relay).start()

        sent[index] = pack(turn, 0, own_part(turn))

        def to_peer(step, carry):
            sent_copy(index, step, me, peer_of(step)).start()
            return carry

        lax.fori_loop(1, half, to_peer, 0)
        got[index, me] = sent[index, 0]

    table_copy(spot // relays, my_relay).start()
    prepare(0, table)
    for turn in range(AHEAD):
        send(turn)
    for load in loads:
        load.wait()

    def pass_on(turn):
        index = index_of(turn)
        for u in range(2):
            source = away_of(u)
            if turn == 0:
                table_copy(u, source).wait_recv()
                prepare(1 + u, table_got.at[u])
            raw_copy(turn, u, source).wait_recv()

            passed[index, u] = pack(turn, 1 + u, raw[u, index])

            def to_peer(step, carry):
                passed_copy(index, u, step, source, peer_of(step)).start()
                return carry

            lax.fori_loop(1, half, to_peer, 0)
            got[index, source] = passed[index, u, 0]

    def receive(turn):
        index = index_of(turn)

        def from_peer(step, carry):
            source = peer_of(step)
            sent_copy(index, step, source, source).wait_recv()
            return carry

        def from_away(step, carry):
            source = away + step

            def wait():
                passed_copy(index, 0, 0, source, source).wait_recv()

            pl.when(home_relays + step % relays != me)(wait)
            return carry

        lax.fori_loop(1, half, from_peer, 0)
        lax.fori_loop(0, half, from_away, 0)

    def share(to, slot):
        return pltpu.make_async_remote_copy(
            src_ref=w_sent.at[to],
            dst_ref=w_got.at[slot],
            send_sem=w_send.at[to],
            recv_sem=w_recv.at[slot],
            device_id={"dp": to},
        )

    flat = experts * slots
    hidden = act.shape[1]

    def down_part(turn):
        piece = piece_of(turn % pieces)
        down = lax.dot_general(
            act[...],
            got[index_of(turn)].reshape(flat, width),
            BY_ROWS,
            preferred_element_type=jnp.float32,
        ).astype(jnp.bfloat16)
        last = turn == turns - 1
        for u in range(per_piece):
            to = piece * per_piece + u
            w_sent[to] = down[:, u * columns : (u + 1) * columns]
            if not last:
                share(to, group).start()
            elif per_piece > 1:
                pl.when(to != group)(lambda: share(to, group).start())

    for turn in range(turns):
        pl.when(is_relay)(functools.partial(pass_on, turn))
        if turn + AHEAD < turns:
            send(turn + AHEAD)
        receive(turn)
        weights = w_in if turn < pieces else w_out
        part = lax.dot_general(
            got[index_of(turn)].reshape(flat, width),
            weights[piece_of(turn % pieces)],
            BY_COLS,
            preferred_element_type=jnp.float32,
        )
        if turn % pieces > 0:
            part = part + sums[...]
        if turn == pieces - 1:
            sig = 1.0 / (1.0 + jnp.exp(-part))
            act[...] = (part * sig).astype(jnp.bfloat16)
            slope[...] = sig * (1.0 + part * (1.0 - sig))
        elif turn == turns - 1:
            dpre[...] = (part * slope[...]).astype(jnp.bfloat16).reshape(experts, slots, hidden)
        else:
            sums[...] = part
        if pieces <= turn < turns - 1:
            down_part(turn)

    def rows_back(first, p):
        block = dpre[pl.ds(first, half)].reshape(half * slots, hidden)
        return (
            jnp.dot(block, w_in[p], preferred_element_type=jnp.float32)
            .astype(jnp.bfloat16)
            .reshape(half, slots, width)
        )

    def relay_copy(p, spot_to, slot, at, to):
        return remote(
            sent_away.at[p, spot_to],
            relay_back.at[p, slot, at],
            away_send.at[p, spot_to],
            relay_recv.at[p, slot, at],
            to,
        )

    def back_copy(p, spot_to, at, to):
        return remote(
            sent_home.at[p, spot_to],
            got_back.at[p, at],
            home_send.at[p, spot_to],
            back_recv.at[p, at],
            to,
        )

    def far_copy(p, u, to):
        return remote(
            relay_sum.at[p, u], far.at[p], sum_send.at[p, u], far_recv.at[p], to
        )

    for p in range(pieces):
        sent_away[p] = rows_back(away, p)

        def back_away(step, carry):
            relay = home_relays + step % relays
            slot = step // relays

            def keep():
                relay_back[p, slot, 0] = sent_away[p, step]

            def hand():
                at = (spot + half - (relay - home)) % half
                relay_copy(p, step, slot, at, relay).start()

            pl.when(relay == me)(keep)
            pl.when(relay != me)(hand)
            return carry

        lax.fori_loop(0, half, back_away, 0)

    for p in range(pieces):
        sent_home[p] = rows_back(home, p)

        def back_home(step, carry):
            back_copy(p, (spot + step) % half, half - step, peer_of(step)).start()
            return carry

        lax.fori_loop(1, half, back_home, 0)
        got_back[p, 0] = sent_home[p, spot]

    def combine(k, block):
        return lax.dot_general(
            pick_of(k),
            block.reshape(half * slots, width),
            BY_ROWS,
            preferred_element_type=jnp.float32,
        )

    def relay_sums():
        for p in range(pieces):
            for u in range(2):

                def arrive(step, carry):
                    relay_copy(p, 0, u, step, me + 1 - 2 * (me % 2)).wait_recv()
                    return carry

                lax.fori_loop(1, half, arrive, 0)
                relay_sum[p, u] = combine(1 + u, relay_back[p, u]).astype(jnp.bfloat16)
                far_copy(p, u, away_of(u)).start()

    pl.when(is_relay)(relay_sums)
    down_part(turns - 1)

    w_own[...] = w_sent[group].astype(jnp.float32)

    def gather(step, carry):
        source = (group + step) % groups
        share(source, source).wait_recv()
        w_own[...] += w_got[source].astype(jnp.float32)
        return carry

    lax.fori_loop(1, groups, gather, 0)
    grad_w[...] = w_own[...].astype(jnp.bfloat16)

    for p in range(pieces):

        def take_back(step, carry):
            back_copy(p, 0, step, peer_of(step)).wait_recv()
            return carry

        lax.fori_loop(1, half, take_back, 0)
        near = combine(0, got_back[p])
        far_copy(p, 0, my_relay).wait_recv()
        grad_tokens[:, p * width : (p + 1) * width] = (near + far[p].astype(jnp.float32)).astype(
            jnp.bfloat16
        )

    table_copy(0, my_relay).wait_send()
    for turn in range(turns):
        index = index_of(turn)
        raw_copy(turn, 0, my_relay).wait_send()

        def drain_sent(step, carry):
            sent_copy(index, step, me, peer_of(step)).wait_send()
            return carry

        def drain_passed(step, carry):
            for u in range(2):
                passed_copy(index, u, step, me, peer_of(step)).wait_send()
            return carry

        lax.fori_loop(1, half, drain_sent, 0)

        def drain_all_passed():
            lax.fori_loop(1, half, drain_passed, 0)

        pl.when(is_relay)(drain_all_passed)

    def drain_away(step, carry):
        relay = home_relays + step % relays

        def wait():
            for p in range(pieces):
                relay_copy(p, step, 0, 0, relay).wait_send()

        pl.when(relay != me)(wait)
        return carry

    def drain_home(step, carry):
        for p in range(pieces):
            back_copy(p, (spot + step) % half, half - step, peer_of(step)).wait_send()
        return carry

    def drain_sums():
        for p in range(pieces):
            for u in range(2):
                far_copy(p, u, away_of(u)).wait_send()

    def drain_group(step, carry):
        share((group + step) % groups, group).wait_send()
        return carry

    lax.fori_loop(0, half, drain_away, 0)
    lax.fori_loop(1, half, drain_home, 0)
    pl.when(is_relay)(drain_sums)
    lax.fori_loop(1, groups, drain_group, 0)


def hand_over(first, second, first_out, second_out, first_held, second_held, sems):
    steps = []
    for ref, held, out, which in (
        (first, first_held, first_out, 0),
        (second, second_held, second_out, 1),
    ):
        steps.append(
            (
                pltpu.make_async_copy(ref, held, sems.at[0, which]),
                pltpu.make_async_copy(held, out, sems.at[1, which]),
            )
        )
    for load, _ in steps:
        load.start()
    for load, store in steps:
        load.wait()
        store.start()
    for _, store in steps:
        store.wait()


def per_device(tokens, cotangent, gates, expert_ids, w_in, w_out):
    rows, width = tokens.shape
    hidden = w_out.shape[1]
    experts, groups = lax.axis_size("expert"), lax.axis_size("dp")
    capacity = 5 * rows * expert_ids.shape[1] // (4 * experts)
    slots = -(-capacity // 8) * 8
    columns = width // groups
    pieces = 4 if groups % 4 == 0 else 1
    half, turns, part = experts // 2, 2 * pieces, width // pieces
    shares = pltpu.VMEM((groups, hidden, columns), jnp.bfloat16)
    vmem = pl.BlockSpec(memory_space=pltpu.VMEM)
    anywhere = pl.BlockSpec(memory_space=pl.ANY)
    multiplies = experts * slots * width * hidden
    outs = (
        jax.ShapeDtypeStruct((rows, width), jnp.bfloat16),
        jax.ShapeDtypeStruct((hidden, columns), jnp.bfloat16),
    )
    results = pl.pallas_call(
        functools.partial(layer_kernel, experts, groups, pieces),
        out_shape=outs,
        in_specs=[vmem] * 4 + [anywhere] * 2,
        out_specs=(vmem, vmem),
        scratch_shapes=[
            pltpu.VMEM((pieces, hidden, part), jnp.bfloat16),
            pltpu.VMEM((pieces, hidden, part), jnp.bfloat16),
            pltpu.VMEM((2, experts, rows), jnp.float32),
            pltpu.VMEM((2, 2, experts, rows), jnp.float32),
            pltpu.VMEM((3, half, slots, rows), jnp.bfloat16),
            pltpu.VMEM((3, half, slots, 1), jnp.float32),
            pltpu.VMEM((2, turns, rows, part), jnp.bfloat16),
            pltpu.VMEM((turns, half, slots, part), jnp.bfloat16),
            pltpu.VMEM((turns, 2, half, slots, part), jnp.bfloat16),
            pltpu.VMEM((turns, experts, slots, part), jnp.bfloat16),
            pltpu.VMEM((experts * slots, hidden), jnp.float32),
            pltpu.VMEM((experts * slots, hidden), jnp.bfloat16),
            pltpu.VMEM((experts * slots, hidden), jnp.float32),
            pltpu.VMEM((experts, slots, hidden), jnp.bfloat16),
            pltpu.VMEM((pieces, half, slots, part), jnp.bfloat16),
            pltpu.VMEM((pieces, half, slots, part), jnp.bfloat16),
            pltpu.VMEM((pieces, half, slots, part), jnp.bfloat16),
            pltpu.VMEM((pieces, 2, half, slots, part), jnp.bfloat16),
            pltpu.VMEM((pieces, 2, rows, part), jnp.bfloat16),
            pltpu.VMEM((pieces, rows, part), jnp.bfloat16),
            pltpu.VMEM((hidden, columns), jnp.float32),
            shares,
            shares,
            pltpu.SemaphoreType.DMA((2, pieces)),
            pltpu.SemaphoreType.DMA((3,)),
            pltpu.SemaphoreType.DMA((turns,)),
            pltpu.SemaphoreType.DMA((2, turns)),
            pltpu.SemaphoreType.DMA((turns, half)),
            pltpu.SemaphoreType.DMA((turns, 2, half)),
            pltpu.SemaphoreType.DMA((turns, experts)),
            pltpu.SemaphoreType.DMA((pieces, half)),
            pltpu.SemaphoreType.DMA((pieces, half)),
            pltpu.SemaphoreType.DMA((pieces, half)),
            pltpu.SemaphoreType.DMA((pieces, 2, half)),
            pltpu.SemaphoreType.DMA((pieces, 2)),
            pltpu.SemaphoreType.DMA((pieces,)),
            pltpu.SemaphoreType.DMA((groups,)),
            pltpu.SemaphoreType.DMA((groups,)),
        ],
        compiler_params=pltpu.CompilerParams(
            collective_id=0, has_side_effects=True, vmem_limit_bytes=56 * 1024 * 1024
        ),
        cost_estimate=pl.CostEstimate(
            flops=8 * multiplies, bytes_accessed=4 * hidden * width, transcendentals=0
        ),
    )(
        tokens,
        cotangent,
        gates.T,
        expert_ids.T,
        jnp.swapaxes(w_in[0], 0, 1),
        w_out[0],
    )
    grad_tokens, grad_w = pl.pallas_call(
        hand_over,
        out_shape=outs,
        in_specs=[anywhere] * 2,
        out_specs=(anywhere, anywhere),
        scratch_shapes=[
            pltpu.VMEM(outs[0].shape, jnp.bfloat16),
            pltpu.VMEM(outs[1].shape, jnp.bfloat16),
            pltpu.SemaphoreType.DMA((2, 2)),
        ],
        compiler_params=pltpu.CompilerParams(vmem_limit_bytes=56 * 1024 * 1024),
    )(*results)
    return grad_tokens, grad_w[None]


def solution(mesh):
    split = P(("expert", "dp"), None)
    whole = P("expert", None, None)
    return jax.shard_map(
        per_device,
        mesh=mesh,
        in_specs=(split, split, split, split, whole, whole),
        out_specs=(split, P("expert", None, "dp")),
        check_vma=False,
    )
```

```python
import functools

import jax
import jax.numpy as jnp
from jax import lax
from jax.experimental import pallas as pl
from jax.experimental.pallas import tpu as pltpu
from jax.sharding import PartitionSpec as P

BY_COLS = (((1,), (1,)), ((), ()))
BY_ROWS = (((0,), (0,)), ((), ()))


AHEAD = 5


def layer_kernel(
    experts, groups, pieces, tokens, cotangent, gates, ids, w_in_hbm, w_out_hbm, grad_tokens,
    grad_w, w_in, w_out, table, table_got, picks, weights_of, raw, sent, passed, got, sums,
    act, slope, dpre, sent_home, sent_away, got_back, relay_back, relay_sum, far, w_own, w_sent, w_got, load_sems,
    table_sems, raw_send, raw_recv, sent_sems, passed_sems, got_sems, home_send, away_send,
    back_recv, relay_recv, sum_send, far_recv, w_send, w_recv,
):
    me = lax.axis_index("expert")
    group = lax.axis_index("dp")
    half = experts // 2
    relays = half // 2
    slots = got.shape[3]
    rows = tokens.shape[0]
    columns = grad_w.shape[1]
    per_piece = groups // pieces
    width = per_piece * columns
    stage = 2 * pieces
    turns = 2 * stage
    my_piece = group // per_piece

    loads = [
        pltpu.make_async_copy(hbm.at[:, pl.ds(p * width, width)], held.at[p], load_sems.at[k, p])
        for k, (hbm, held) in enumerate(((w_in_hbm, w_in), (w_out_hbm, w_out)))
        for p in range(pieces)
    ]
    for load in loads:
        load.start()

    barrier = pltpu.get_barrier_semaphore()

    def greet_expert(step, carry):
        pl.semaphore_signal(barrier, inc=1, device_id={"expert": (me + step) % experts})
        return carry

    def greet_group(step, carry):
        pl.semaphore_signal(barrier, inc=1, device_id={"dp": (group + step) % groups})
        return carry

    lax.fori_loop(1, experts, greet_expert, 0)
    lax.fori_loop(1, groups, greet_group, 0)

    side = me // half
    spot = me % half
    home = side * half
    away = (1 - side) * half
    mine = spot % 2
    number = spot % relays
    is_relay = spot // relays == 1 - side
    my_relay = side * relays + (1 - side) * half + spot // 2
    home_relays = (1 - side) * relays + side * half

    def peer_of(step):
        return home + (spot + step) % half

    def away_of(u):
        return away + 2 * number + u

    def piece_of(turn):
        return (my_piece + 1 + turn) % pieces

    def index_of(turn):
        return (turn % stage // pieces) * pieces + piece_of(turn % pieces)

    def entry(source):
        return source // half * relays + source % half // 2

    def remote(source, dest, send_sem, recv_sem, to):
        return pltpu.make_async_remote_copy(
            src_ref=source,
            dst_ref=dest,
            send_sem=send_sem,
            recv_sem=recv_sem,
            device_id={"expert": to},
        )

    def table_copy(slot, to):
        return remote(table, table_got.at[slot], table_sems.at[2], table_sems.at[slot], to)

    def raw_copy(turn, slot, to):
        part = tokens if turn % stage < pieces else cotangent
        start = pl.multiple_of(piece_of(turn % pieces) * width, width)
        index = index_of(turn)
        return remote(
            part.at[:, pl.ds(start, width)],
            raw.at[slot, index],
            raw_send.at[index],
            raw_recv.at[slot, index],
            to,
        )

    def sent_copy(index, step, slot, to):
        return remote(
            sent.at[index, step],
            got.at[index, slot % 2, entry(slot)],
            sent_sems.at[index, step],
            got_sems.at[index, slot],
            to,
        )

    def passed_copy(index, u, step, slot, to):
        return remote(
            passed.at[index, u, step],
            got.at[index, slot % 2, entry(slot)],
            passed_sems.at[index, u, step],
            got_sems.at[index, slot],
            to,
        )

    expert_of = lax.broadcasted_iota(jnp.int32, (experts, rows), 0)
    chosen = jnp.zeros((experts, rows), jnp.float32)
    gain = jnp.zeros((experts, rows), jnp.float32)
    for k in range(ids.shape[0]):
        hit = expert_of == ids[k : k + 1, :]
        chosen = chosen + jnp.where(hit, 1.0, 0.0)
        gain = gain + jnp.where(hit, gates[k : k + 1, :], 0.0)
    earlier = jnp.where(
        lax.broadcasted_iota(jnp.int32, (rows, rows), 0)
        < lax.broadcasted_iota(jnp.int32, (rows, rows), 1),
        1.0,
        0.0,
    ).astype(jnp.bfloat16)
    place = jnp.dot(chosen.astype(jnp.bfloat16), earlier, preferred_element_type=jnp.float32)
    table[0] = jnp.where(chosen > 0.0, place, -1.0)
    table[1] = gain
    slot_number = lax.broadcasted_iota(jnp.int32, (slots, rows), 0).astype(jnp.float32)

    def prepare(k, held):
        for step in range(half):
            expert = peer_of(step)
            match = slot_number == held[0, pl.ds(expert, 1), :]
            picks[k, step] = jnp.where(match, 1.0, 0.0).astype(jnp.bfloat16)
            gain_row = held[1, pl.ds(expert, 1), :]
            weights_of[k, step] = jnp.sum(
                jnp.where(match, gain_row, 0.0), axis=1, keepdims=True
            )

    def pick_of(k):
        return picks[k].reshape(half * slots, rows)

    def pack(turn, k, part):
        out = jnp.dot(pick_of(k), part, preferred_element_type=jnp.float32)
        if turn % stage >= pieces:
            out = out * weights_of[k].reshape(half * slots, 1)
        return out.astype(jnp.bfloat16).reshape(half, slots, width)

    def own_part(turn):
        part = tokens if turn % stage < pieces else cotangent
        return part[:, pl.ds(pl.multiple_of(piece_of(turn % pieces) * width, width), width)]

    pl.semaphore_wait(barrier, experts + groups - 2)

    def send(turn):
        index = index_of(turn)
        raw_copy(turn, mine, my_relay).start()

        sent[index] = pack(turn, 0, own_part(turn))

        def to_peer(step, carry):
            sent_copy(index, step, me, peer_of(step)).start()
            return carry

        lax.fori_loop(1, half, to_peer, 0)
        got[index, mine, entry(me)] = sent[index, 0]

    table_copy(mine, my_relay).start()
    prepare(0, table)
    for turn in range(AHEAD):
        pl.when(mine == turn // stage)(functools.partial(send, turn))
    for load in loads:
        load.wait()

    def pass_on(turn):
        index = index_of(turn)
        u = turn // stage
        source = away_of(u)
        if turn % stage == 0:
            table_copy(u, source).wait_recv()
            prepare(1 + u, table_got.at[u])
        raw_copy(turn, u, source).wait_recv()
        passed[index, u] = pack(turn, 1 + u, raw[u, index])

        def to_peer(step, carry):
            passed_copy(index, u, step, source, peer_of(step)).start()
            return carry

        lax.fori_loop(1, half, to_peer, 0)
        got[index, u, entry(source)] = passed[index, u, 0]

    def receive(turn):
        index = index_of(turn)
        u = turn // stage

        def from_peer(step, carry):
            source = peer_of(step)

            def wait():
                sent_copy(index, step, source, source).wait_recv()

            pl.when(source % 2 == u)(wait)
            return carry

        def from_away(step, carry):
            source = away + 2 * step + u

            def wait():
                passed_copy(index, 0, 0, source, source).wait_recv()

            pl.when(home_relays + step != me)(wait)
            return carry

        lax.fori_loop(1, half, from_peer, 0)
        lax.fori_loop(0, relays, from_away, 0)

    def share(to, slot):
        return pltpu.make_async_remote_copy(
            src_ref=w_sent.at[to],
            dst_ref=w_got.at[slot],
            send_sem=w_send.at[to],
            recv_sem=w_recv.at[slot],
            device_id={"dp": to},
        )

    flat = half * slots
    hidden = act.shape[1]

    def down_part(turn):
        piece = piece_of(turn % pieces)
        down = lax.dot_general(
            act[...],
            got[index_of(turn)].reshape(2 * flat, width),
            BY_ROWS,
            preferred_element_type=jnp.float32,
        ).astype(jnp.bfloat16)
        last = turn == turns - 1
        for u in range(per_piece):
            to = piece * per_piece + u
            w_sent[to] = down[:, u * columns : (u + 1) * columns]
            if not last:
                share(to, group).start()
            elif per_piece > 1:
                pl.when(to != group)(lambda: share(to, group).start())

    def rows_back(u, first, p):
        block = dpre[u, pl.ds(first, relays)].reshape(relays * slots, hidden)
        return (
            jnp.dot(block, w_in[p], preferred_element_type=jnp.float32)
            .astype(jnp.bfloat16)
            .reshape(relays, slots, width)
        )

    def relay_copy(p, u, step, at, to):
        return remote(
            sent_away.at[p, u, step],
            relay_back.at[p, u, at],
            away_send.at[p, u, step],
            relay_recv.at[p, u, at],
            to,
        )

    def back_copy(p, u, step, at, to):
        return remote(
            sent_home.at[p, u, step],
            got_back.at[p, at],
            home_send.at[p, u, step],
            back_recv.at[p, at],
            to,
        )

    def far_copy(p, u, to):
        return remote(
            relay_sum.at[p, u], far.at[p], sum_send.at[p, u], far_recv.at[p], to
        )

    def away_rows(u):
        for p in range(pieces):
            sent_away[p, u] = rows_back(u, (1 - side) * relays, p)

            def back_away(step, carry):
                relay = home_relays + step

                def keep():
                    relay_back[p, u, 0] = sent_away[p, u, step]

                def hand():
                    at = (spot + half - (relay - home)) % half
                    relay_copy(p, u, step, at, relay).start()

                pl.when(relay == me)(keep)
                pl.when(relay != me)(hand)
                return carry

            lax.fori_loop(0, relays, back_away, 0)

    def home_rows(u):
        for p in range(pieces):
            sent_home[p, u] = rows_back(u, side * relays, p)

            def back_home(step, carry):
                to = 2 * step + u

                def keep():
                    got_back[p, 0] = sent_home[p, u, step]

                def hand():
                    back_copy(p, u, step, (spot + half - to) % half, home + to).start()

                pl.when(to == spot)(keep)
                pl.when(to != spot)(hand)
                return carry

            lax.fori_loop(0, relays, back_home, 0)

    def combine(k, block):
        return lax.dot_general(
            pick_of(k),
            block.reshape(half * slots, width),
            BY_ROWS,
            preferred_element_type=jnp.float32,
        )

    def relay_sums(u):
        for p in range(pieces):

            def arrive(step, carry):
                relay_copy(p, u, 0, step, peer_of(step)).wait_recv()
                return carry

            lax.fori_loop(1, half, arrive, 0)
            relay_sum[p, u] = combine(1 + u, relay_back[p, u]).astype(jnp.bfloat16)
            far_copy(p, u, away_of(u)).start()

    for turn in range(turns):
        u = turn // stage
        pl.when(is_relay)(functools.partial(pass_on, turn))
        later = turn + AHEAD
        if later < turns:
            pl.when(mine == later // stage)(functools.partial(send, later))
        if turn == turns - 1:
            pl.when(is_relay)(functools.partial(relay_sums, 0))
        receive(turn)
        weights = w_in if turn % stage < pieces else w_out
        part = lax.dot_general(
            got[index_of(turn), u].reshape(flat, width),
            weights[piece_of(turn % pieces)],
            BY_COLS,
            preferred_element_type=jnp.float32,
        )
        if turn % pieces > 0:
            part = part + sums[...]
        if turn % stage == pieces - 1:
            sig = 1.0 / (1.0 + jnp.exp(-part))
            act[u * flat : (u + 1) * flat] = (part * sig).astype(jnp.bfloat16)
            slope[...] = sig * (1.0 + part * (1.0 - sig))
        elif turn % stage == stage - 1:
            dpre[u] = (part * slope[...]).astype(jnp.bfloat16).reshape(half, slots, hidden)
        else:
            sums[...] = part
        if stage + pieces <= turn < turns - 1:
            down_part(turn)
        if turn == stage + pieces:
            away_rows(0)
        if turn == stage + pieces + 1:
            home_rows(0)

    away_rows(1)
    home_rows(1)
    pl.when(is_relay)(functools.partial(relay_sums, 1))
    down_part(turns - 1)

    w_own[...] = w_sent[group].astype(jnp.float32)

    def gather(step, carry):
        source = (group + step) % groups
        share(source, source).wait_recv()
        w_own[...] += w_got[source].astype(jnp.float32)
        return carry

    lax.fori_loop(1, groups, gather, 0)
    grad_w[...] = w_own[...].astype(jnp.bfloat16)

    for p in range(pieces):

        def take_back(step, carry):
            back_copy(p, 0, 0, step, peer_of(step)).wait_recv()
            return carry

        lax.fori_loop(1, half, take_back, 0)
        near = combine(0, got_back[p])
        far_copy(p, 0, my_relay).wait_recv()
        grad_tokens[:, p * width : (p + 1) * width] = (near + far[p].astype(jnp.float32)).astype(
            jnp.bfloat16
        )

    table_copy(0, my_relay).wait_send()
    for turn in range(stage):
        index = index_of(turn)
        raw_copy(turn, 0, my_relay).wait_send()

        def drain_sent(step, carry):
            sent_copy(index, step, me, peer_of(step)).wait_send()
            return carry

        def drain_passed(step, carry):
            for u in range(2):
                passed_copy(index, u, step, me, peer_of(step)).wait_send()
            return carry

        lax.fori_loop(1, half, drain_sent, 0)

        def drain_all_passed():
            lax.fori_loop(1, half, drain_passed, 0)

        pl.when(is_relay)(drain_all_passed)

    def drain_back(step, carry):
        for u in range(2):

            def wait_away():
                for p in range(pieces):
                    relay_copy(p, u, step, 0, home_relays + step).wait_send()

            def wait_home():
                for p in range(pieces):
                    back_copy(p, u, step, 0, home + 2 * step + u).wait_send()

            pl.when(home_relays + step != me)(wait_away)
            pl.when(2 * step + u != spot)(wait_home)
        return carry

    def drain_sums():
        for p in range(pieces):
            for u in range(2):
                far_copy(p, u, away_of(u)).wait_send()

    def drain_group(step, carry):
        share((group + step) % groups, group).wait_send()
        return carry

    lax.fori_loop(0, relays, drain_back, 0)
    pl.when(is_relay)(drain_sums)
    lax.fori_loop(1, groups, drain_group, 0)


def hand_over(first, second, first_out, second_out, first_held, second_held, sems):
    steps = []
    for ref, held, out, which in (
        (first, first_held, first_out, 0),
        (second, second_held, second_out, 1),
    ):
        steps.append(
            (
                pltpu.make_async_copy(ref, held, sems.at[0, which]),
                pltpu.make_async_copy(held, out, sems.at[1, which]),
            )
        )
    for load, _ in steps:
        load.start()
    for load, store in steps:
        load.wait()
        store.start()
    for _, store in steps:
        store.wait()


def per_device(tokens, cotangent, gates, expert_ids, w_in, w_out):
    rows, width = tokens.shape
    hidden = w_out.shape[1]
    experts, groups = lax.axis_size("expert"), lax.axis_size("dp")
    capacity = 5 * rows * expert_ids.shape[1] // (4 * experts)
    slots = -(-capacity // 8) * 8
    columns = width // groups
    pieces = 4 if groups % 4 == 0 else 1
    half, turns, part = experts // 2, 2 * pieces, width // pieces
    shares = pltpu.VMEM((groups, hidden, columns), jnp.bfloat16)
    vmem = pl.BlockSpec(memory_space=pltpu.VMEM)
    anywhere = pl.BlockSpec(memory_space=pl.ANY)
    multiplies = experts * slots * width * hidden
    outs = (
        jax.ShapeDtypeStruct((rows, width), jnp.bfloat16),
        jax.ShapeDtypeStruct((hidden, columns), jnp.bfloat16),
    )
    results = pl.pallas_call(
        functools.partial(layer_kernel, experts, groups, pieces),
        out_shape=outs,
        in_specs=[vmem] * 4 + [anywhere] * 2,
        out_specs=(vmem, vmem),
        scratch_shapes=[
            pltpu.VMEM((pieces, hidden, part), jnp.bfloat16),
            pltpu.VMEM((pieces, hidden, part), jnp.bfloat16),
            pltpu.VMEM((2, experts, rows), jnp.float32),
            pltpu.VMEM((2, 2, experts, rows), jnp.float32),
            pltpu.VMEM((3, half, slots, rows), jnp.bfloat16),
            pltpu.VMEM((3, half, slots, 1), jnp.float32),
            pltpu.VMEM((2, turns, rows, part), jnp.bfloat16),
            pltpu.VMEM((turns, half, slots, part), jnp.bfloat16),
            pltpu.VMEM((turns, 2, half, slots, part), jnp.bfloat16),
            pltpu.VMEM((turns, 2, half, slots, part), jnp.bfloat16),
            pltpu.VMEM((half * slots, hidden), jnp.float32),
            pltpu.VMEM((experts * slots, hidden), jnp.bfloat16),
            pltpu.VMEM((half * slots, hidden), jnp.float32),
            pltpu.VMEM((2, half, slots, hidden), jnp.bfloat16),
            pltpu.VMEM((pieces, 2, half // 2, slots, part), jnp.bfloat16),
            pltpu.VMEM((pieces, 2, half // 2, slots, part), jnp.bfloat16),
            pltpu.VMEM((pieces, half, slots, part), jnp.bfloat16),
            pltpu.VMEM((pieces, 2, half, slots, part), jnp.bfloat16),
            pltpu.VMEM((pieces, 2, rows, part), jnp.bfloat16),
            pltpu.VMEM((pieces, rows, part), jnp.bfloat16),
            pltpu.VMEM((hidden, columns), jnp.float32),
            shares,
            shares,
            pltpu.SemaphoreType.DMA((2, pieces)),
            pltpu.SemaphoreType.DMA((3,)),
            pltpu.SemaphoreType.DMA((turns,)),
            pltpu.SemaphoreType.DMA((2, turns)),
            pltpu.SemaphoreType.DMA((turns, half)),
            pltpu.SemaphoreType.DMA((turns, 2, half)),
            pltpu.SemaphoreType.DMA((turns, experts)),
            pltpu.SemaphoreType.DMA((pieces, 2, half // 2)),
            pltpu.SemaphoreType.DMA((pieces, 2, half // 2)),
            pltpu.SemaphoreType.DMA((pieces, half)),
            pltpu.SemaphoreType.DMA((pieces, 2, half)),
            pltpu.SemaphoreType.DMA((pieces, 2)),
            pltpu.SemaphoreType.DMA((pieces,)),
            pltpu.SemaphoreType.DMA((groups,)),
            pltpu.SemaphoreType.DMA((groups,)),
        ],
        compiler_params=pltpu.CompilerParams(
            collective_id=0, has_side_effects=True, vmem_limit_bytes=56 * 1024 * 1024
        ),
        cost_estimate=pl.CostEstimate(
            flops=8 * multiplies, bytes_accessed=4 * hidden * width, transcendentals=0
        ),
    )(
        tokens,
        cotangent,
        gates.T,
        expert_ids.T,
        jnp.swapaxes(w_in[0], 0, 1),
        w_out[0],
    )
    grad_tokens, grad_w = pl.pallas_call(
        hand_over,
        out_shape=outs,
        in_specs=[anywhere] * 2,
        out_specs=(anywhere, anywhere),
        scratch_shapes=[
            pltpu.VMEM(outs[0].shape, jnp.bfloat16),
            pltpu.VMEM(outs[1].shape, jnp.bfloat16),
            pltpu.SemaphoreType.DMA((2, 2)),
        ],
        compiler_params=pltpu.CompilerParams(vmem_limit_bytes=56 * 1024 * 1024),
    )(*results)
    return grad_tokens, grad_w[None]


def solution(mesh):
    split = P(("expert", "dp"), None)
    whole = P("expert", None, None)
    return jax.shard_map(
        per_device,
        mesh=mesh,
        in_specs=(split, split, split, split, whole, whole),
        out_specs=(split, P("expert", None, "dp")),
        check_vma=False,
    )
```

```python
import functools

import jax
import jax.numpy as jnp
from jax import lax
from jax.experimental import pallas as pl
from jax.experimental.pallas import tpu as pltpu
from jax.sharding import PartitionSpec as P

BY_COLS = (((1,), (1,)), ((), ()))
BY_ROWS = (((0,), (0,)), ((), ()))


AHEAD = 3


def layer_kernel(
    experts, groups, pieces, tokens, cotangent, gates, ids, w_in_hbm, w_out_hbm, grad_tokens,
    grad_w, w_in, w_out, table, table_got, picks, weights_of, raw, sent, passed, got, sums,
    act, slope, dpre, sent_home, sent_away, got_back, relay_back, relay_sum, far, w_own, w_sent, w_got, load_sems,
    table_sems, raw_send, raw_recv, sent_sems, passed_sems, got_sems, home_send, away_send,
    back_recv, relay_recv, sum_send, far_recv, w_send, w_recv,
):
    me = lax.axis_index("expert")
    group = lax.axis_index("dp")
    half = experts // 2
    relays = half // 2
    slots = got.shape[2]
    rows = tokens.shape[0]
    columns = grad_w.shape[1]
    per_piece = groups // pieces
    width = per_piece * columns
    turns = 2 * pieces
    my_piece = group // per_piece

    loads = [
        pltpu.make_async_copy(hbm.at[:, pl.ds(p * width, width)], held.at[p], load_sems.at[k, p])
        for k, (hbm, held) in enumerate(((w_in_hbm, w_in), (w_out_hbm, w_out)))
        for p in range(pieces)
    ]
    for load in loads:
        load.start()

    barrier = pltpu.get_barrier_semaphore()

    def greet_expert(step, carry):
        pl.semaphore_signal(barrier, inc=1, device_id={"expert": (me + step) % experts})
        return carry

    def greet_group(step, carry):
        pl.semaphore_signal(barrier, inc=1, device_id={"dp": (group + step) % groups})
        return carry

    lax.fori_loop(1, experts, greet_expert, 0)
    lax.fori_loop(1, groups, greet_group, 0)

    side = me // half
    spot = me % half
    home = side * half
    away = (1 - side) * half
    number = spot % relays
    is_relay = spot // relays == 1 - side
    my_relay = side * relays + (1 - side) * half + number
    home_relays = (1 - side) * relays + side * half

    def peer_of(step):
        return home + (spot + step) % half

    def away_of(u):
        return away + number + u * relays

    def piece_of(turn):
        return (my_piece + 1 + turn) % pieces

    def index_of(turn):
        return (turn // pieces) * pieces + piece_of(turn % pieces)

    def remote(source, dest, send_sem, recv_sem, to):
        return pltpu.make_async_remote_copy(
            src_ref=source,
            dst_ref=dest,
            send_sem=send_sem,
            recv_sem=recv_sem,
            device_id={"expert": to},
        )

    def table_copy(slot, to):
        return remote(table, table_got.at[slot], table_sems.at[2], table_sems.at[slot], to)

    def raw_copy(turn, slot, to):
        part = tokens if turn < pieces else cotangent
        start = pl.multiple_of(piece_of(turn % pieces) * width, width)
        index = index_of(turn)
        return remote(
            part.at[:, pl.ds(start, width)],
            raw.at[slot, index],
            raw_send.at[index],
            raw_recv.at[slot, index],
            to,
        )

    def sent_copy(index, step, slot, to):
        return remote(
            sent.at[index, step],
            got.at[index, slot],
            sent_sems.at[index, step],
            got_sems.at[index, slot],
            to,
        )

    def passed_copy(index, u, step, slot, to):
        return remote(
            passed.at[index, u, step],
            got.at[index, slot],
            passed_sems.at[index, u, step],
            got_sems.at[index, slot],
            to,
        )

    expert_of = lax.broadcasted_iota(jnp.int32, (experts, rows), 0)
    chosen = jnp.zeros((experts, rows), jnp.float32)
    gain = jnp.zeros((experts, rows), jnp.float32)
    for k in range(ids.shape[0]):
        hit = expert_of == ids[k : k + 1, :]
        chosen = chosen + jnp.where(hit, 1.0, 0.0)
        gain = gain + jnp.where(hit, gates[k : k + 1, :], 0.0)
    earlier = jnp.where(
        lax.broadcasted_iota(jnp.int32, (rows, rows), 0)
        < lax.broadcasted_iota(jnp.int32, (rows, rows), 1),
        1.0,
        0.0,
    ).astype(jnp.bfloat16)
    place = jnp.dot(chosen.astype(jnp.bfloat16), earlier, preferred_element_type=jnp.float32)
    table[0] = jnp.where(chosen > 0.0, place, -1.0)
    table[1] = gain
    slot_number = lax.broadcasted_iota(jnp.int32, (slots, rows), 0).astype(jnp.float32)

    def prepare(k, held):
        for step in range(half):
            expert = peer_of(step)
            match = slot_number == held[0, pl.ds(expert, 1), :]
            picks[k, step] = jnp.where(match, 1.0, 0.0).astype(jnp.bfloat16)
            gain_row = held[1, pl.ds(expert, 1), :]
            weights_of[k, step] = jnp.sum(
                jnp.where(match, gain_row, 0.0), axis=1, keepdims=True
            )

    def pick_of(k):
        return picks[k].reshape(half * slots, rows)

    def pack(turn, k, part):
        out = jnp.dot(pick_of(k), part, preferred_element_type=jnp.float32)
        if turn >= pieces:
            out = out * weights_of[k].reshape(half * slots, 1)
        return out.astype(jnp.bfloat16).reshape(half, slots, width)

    def own_part(turn):
        part = tokens if turn < pieces else cotangent
        return part[:, pl.ds(pl.multiple_of(piece_of(turn % pieces) * width, width), width)]

    pl.semaphore_wait(barrier, experts + groups - 2)

    def send(turn):
        index = index_of(turn)
        raw_copy(turn, spot // relays, my_relay).start()

        sent[index] = pack(turn, 0, own_part(turn))

        def to_peer(step, carry):
            sent_copy(index, step, me, peer_of(step)).start()
            return carry

        lax.fori_loop(1, half, to_peer, 0)
        got[index, me] = sent[index, 0]

    table_copy(spot // relays, my_relay).start()
    prepare(0, table)
    for turn in range(AHEAD):
        send(turn)
    for load in loads:
        load.wait()

    def pass_on(turn):
        index = index_of(turn)
        for u in range(2):
            source = away_of(u)
            if turn == 0:
                table_copy(u, source).wait_recv()
                prepare(1 + u, table_got.at[u])
            raw_copy(turn, u, source).wait_recv()

            passed[index, u] = pack(turn, 1 + u, raw[u, index])

            def to_peer(step, carry):
                passed_copy(index, u, step, source, peer_of(step)).start()
                return carry

            lax.fori_loop(1, half, to_peer, 0)
            got[index, source] = passed[index, u, 0]

    def receive(turn):
        index = index_of(turn)

        def from_peer(step, carry):
            source = peer_of(step)
            sent_copy(index, step, source, source).wait_recv()
            return carry

        def from_away(step, carry):
            source = away + step

            def wait():
                passed_copy(index, 0, 0, source, source).wait_recv()

            pl.when(home_relays + step % relays != me)(wait)
            return carry

        lax.fori_loop(1, half, from_peer, 0)
        lax.fori_loop(0, half, from_away, 0)

    def share(to, slot):
        return pltpu.make_async_remote_copy(
            src_ref=w_sent.at[to],
            dst_ref=w_got.at[slot],
            send_sem=w_send.at[to],
            recv_sem=w_recv.at[slot],
            device_id={"dp": to},
        )

    flat = experts * slots
    hidden = act.shape[1]

    def down_part(turn):
        piece = piece_of(turn % pieces)
        down = lax.dot_general(
            act[...],
            got[index_of(turn)].reshape(flat, width),
            BY_ROWS,
            preferred_element_type=jnp.float32,
        ).astype(jnp.bfloat16)
        last = turn == turns - 1
        for u in range(per_piece):
            to = piece * per_piece + u
            w_sent[to] = down[:, u * columns : (u + 1) * columns]
            if not last:
                share(to, group).start()
            elif per_piece > 1:
                pl.when(to != group)(lambda: share(to, group).start())

    for turn in range(turns):
        pl.when(is_relay)(functools.partial(pass_on, turn))
        if turn + AHEAD < turns:
            send(turn + AHEAD)
        receive(turn)
        weights = w_in if turn < pieces else w_out
        part = lax.dot_general(
            got[index_of(turn)].reshape(flat, width),
            weights[piece_of(turn % pieces)],
            BY_COLS,
            preferred_element_type=jnp.float32,
        )
        if turn % pieces > 0:
            part = part + sums[...]
        if turn == pieces - 1:
            sig = 1.0 / (1.0 + jnp.exp(-part))
            act[...] = (part * sig).astype(jnp.bfloat16)
            slope[...] = sig * (1.0 + part * (1.0 - sig))
        elif turn == turns - 1:
            dpre[...] = (part * slope[...]).astype(jnp.bfloat16).reshape(experts, slots, hidden)
        else:
            sums[...] = part
        if pieces <= turn < turns - 1:
            down_part(turn)

    def rows_back(first, p):
        block = dpre[pl.ds(first, half)].reshape(half * slots, hidden)
        return (
            jnp.dot(block, w_in[p], preferred_element_type=jnp.float32)
            .astype(jnp.bfloat16)
            .reshape(half, slots, width)
        )

    def relay_copy(p, spot_to, slot, at, to):
        return remote(
            sent_away.at[p, spot_to],
            relay_back.at[p, slot, at],
            away_send.at[p, spot_to],
            relay_recv.at[p, slot, at],
            to,
        )

    def back_copy(p, spot_to, at, to):
        return remote(
            sent_home.at[p, spot_to],
            got_back.at[p, at],
            home_send.at[p, spot_to],
            back_recv.at[p, at],
            to,
        )

    def far_copy(p, u, to):
        return remote(
            relay_sum.at[p, u], far.at[p], sum_send.at[p, u], far_recv.at[p], to
        )

    for p in range(pieces):
        sent_away[p] = rows_back(away, p)

        def back_away(step, carry):
            relay = home_relays + step % relays
            slot = step // relays

            def keep():
                relay_back[p, slot, 0] = sent_away[p, step]

            def hand():
                at = (spot + half - (relay - home)) % half
                relay_copy(p, step, slot, at, relay).start()

            pl.when(relay == me)(keep)
            pl.when(relay != me)(hand)
            return carry

        lax.fori_loop(0, half, back_away, 0)

    def combine(k, block):
        return lax.dot_general(
            pick_of(k),
            block.reshape(half * slots, width),
            BY_ROWS,
            preferred_element_type=jnp.float32,
        )

    def relay_sums():
        for p in range(pieces):
            for u in range(2):

                def arrive(step, carry):
                    relay_copy(p, 0, u, step, me + 1 - 2 * (me % 2)).wait_recv()
                    return carry

                lax.fori_loop(1, half, arrive, 0)
                relay_sum[p, u] = combine(1 + u, relay_back[p, u]).astype(jnp.bfloat16)
                far_copy(p, u, away_of(u)).start()

    pl.when(is_relay)(relay_sums)

    def drain_away(step, carry):
        relay = home_relays + step % relays

        def wait():
            for p in range(pieces):
                relay_copy(p, step, 0, 0, relay).wait_send()

        pl.when(relay != me)(wait)
        return carry

    lax.fori_loop(0, half, drain_away, 0)

    for p in range(pieces):
        sent_home[p] = rows_back(home, p)

        def back_home(step, carry):
            back_copy(p, (spot + step) % half, half - step, peer_of(step)).start()
            return carry

        lax.fori_loop(1, half, back_home, 0)
        got_back[p, 0] = sent_home[p, spot]

    down_part(turns - 1)

    w_own[...] = w_sent[group].astype(jnp.float32)

    def gather(step, carry):
        source = (group + step) % groups
        share(source, source).wait_recv()
        w_own[...] += w_got[source].astype(jnp.float32)
        return carry

    lax.fori_loop(1, groups, gather, 0)
    grad_w[...] = w_own[...].astype(jnp.bfloat16)

    for p in range(pieces):

        def take_back(step, carry):
            back_copy(p, 0, step, peer_of(step)).wait_recv()
            return carry

        lax.fori_loop(1, half, take_back, 0)
        near = combine(0, got_back[p])
        far_copy(p, 0, my_relay).wait_recv()
        grad_tokens[:, p * width : (p + 1) * width] = (near + far[p].astype(jnp.float32)).astype(
            jnp.bfloat16
        )

    table_copy(0, my_relay).wait_send()
    for turn in range(turns):
        index = index_of(turn)
        raw_copy(turn, 0, my_relay).wait_send()

        def drain_sent(step, carry):
            sent_copy(index, step, me, peer_of(step)).wait_send()
            return carry

        def drain_passed(step, carry):
            for u in range(2):
                passed_copy(index, u, step, me, peer_of(step)).wait_send()
            return carry

        lax.fori_loop(1, half, drain_sent, 0)

        def drain_all_passed():
            lax.fori_loop(1, half, drain_passed, 0)

        pl.when(is_relay)(drain_all_passed)

    def drain_home(step, carry):
        for p in range(pieces):
            back_copy(p, (spot + step) % half, half - step, peer_of(step)).wait_send()
        return carry

    def drain_sums():
        for p in range(pieces):
            for u in range(2):
                far_copy(p, u, away_of(u)).wait_send()

    def drain_group(step, carry):
        share((group + step) % groups, group).wait_send()
        return carry

    lax.fori_loop(1, half, drain_home, 0)
    pl.when(is_relay)(drain_sums)
    lax.fori_loop(1, groups, drain_group, 0)


def hand_over(first, second, first_out, second_out, first_held, second_held, sems):
    steps = []
    for ref, held, out, which in (
        (first, first_held, first_out, 0),
        (second, second_held, second_out, 1),
    ):
        steps.append(
            (
                pltpu.make_async_copy(ref, held, sems.at[0, which]),
                pltpu.make_async_copy(held, out, sems.at[1, which]),
            )
        )
    for load, _ in steps:
        load.start()
    for load, store in steps:
        load.wait()
        store.start()
    for _, store in steps:
        store.wait()


def per_device(tokens, cotangent, gates, expert_ids, w_in, w_out):
    rows, width = tokens.shape
    hidden = w_out.shape[1]
    experts, groups = lax.axis_size("expert"), lax.axis_size("dp")
    capacity = 5 * rows * expert_ids.shape[1] // (4 * experts)
    slots = -(-capacity // 8) * 8
    columns = width // groups
    pieces = 4 if groups % 4 == 0 else 1
    half, turns, part = experts // 2, 2 * pieces, width // pieces
    shares = pltpu.VMEM((groups, hidden, columns), jnp.bfloat16)
    vmem = pl.BlockSpec(memory_space=pltpu.VMEM)
    anywhere = pl.BlockSpec(memory_space=pl.ANY)
    multiplies = experts * slots * width * hidden
    outs = (
        jax.ShapeDtypeStruct((rows, width), jnp.bfloat16),
        jax.ShapeDtypeStruct((hidden, columns), jnp.bfloat16),
    )
    results = pl.pallas_call(
        functools.partial(layer_kernel, experts, groups, pieces),
        out_shape=outs,
        in_specs=[vmem] * 4 + [anywhere] * 2,
        out_specs=(vmem, vmem),
        scratch_shapes=[
            pltpu.VMEM((pieces, hidden, part), jnp.bfloat16),
            pltpu.VMEM((pieces, hidden, part), jnp.bfloat16),
            pltpu.VMEM((2, experts, rows), jnp.float32),
            pltpu.VMEM((2, 2, experts, rows), jnp.float32),
            pltpu.VMEM((3, half, slots, rows), jnp.bfloat16),
            pltpu.VMEM((3, half, slots, 1), jnp.float32),
            pltpu.VMEM((2, turns, rows, part), jnp.bfloat16),
            pltpu.VMEM((turns, half, slots, part), jnp.bfloat16),
            pltpu.VMEM((turns, 2, half, slots, part), jnp.bfloat16),
            pltpu.VMEM((turns, experts, slots, part), jnp.bfloat16),
            pltpu.VMEM((experts * slots, hidden), jnp.float32),
            pltpu.VMEM((experts * slots, hidden), jnp.bfloat16),
            pltpu.VMEM((experts * slots, hidden), jnp.float32),
            pltpu.VMEM((experts, slots, hidden), jnp.bfloat16),
            pltpu.VMEM((pieces, half, slots, part), jnp.bfloat16),
            pltpu.VMEM((pieces, half, slots, part), jnp.bfloat16),
            pltpu.VMEM((pieces, half, slots, part), jnp.bfloat16),
            pltpu.VMEM((pieces, 2, half, slots, part), jnp.bfloat16),
            pltpu.VMEM((pieces, 2, rows, part), jnp.bfloat16),
            pltpu.VMEM((pieces, rows, part), jnp.bfloat16),
            pltpu.VMEM((hidden, columns), jnp.float32),
            shares,
            shares,
            pltpu.SemaphoreType.DMA((2, pieces)),
            pltpu.SemaphoreType.DMA((3,)),
            pltpu.SemaphoreType.DMA((turns,)),
            pltpu.SemaphoreType.DMA((2, turns)),
            pltpu.SemaphoreType.DMA((turns, half)),
            pltpu.SemaphoreType.DMA((turns, 2, half)),
            pltpu.SemaphoreType.DMA((turns, experts)),
            pltpu.SemaphoreType.DMA((pieces, half)),
            pltpu.SemaphoreType.DMA((pieces, half)),
            pltpu.SemaphoreType.DMA((pieces, half)),
            pltpu.SemaphoreType.DMA((pieces, 2, half)),
            pltpu.SemaphoreType.DMA((pieces, 2)),
            pltpu.SemaphoreType.DMA((pieces,)),
            pltpu.SemaphoreType.DMA((groups,)),
            pltpu.SemaphoreType.DMA((groups,)),
        ],
        compiler_params=pltpu.CompilerParams(
            collective_id=0, has_side_effects=True, vmem_limit_bytes=56 * 1024 * 1024
        ),
        cost_estimate=pl.CostEstimate(
            flops=8 * multiplies, bytes_accessed=4 * hidden * width, transcendentals=0
        ),
    )(
        tokens,
        cotangent,
        gates.T,
        expert_ids.T,
        jnp.swapaxes(w_in[0], 0, 1),
        w_out[0],
    )
    grad_tokens, grad_w = pl.pallas_call(
        hand_over,
        out_shape=outs,
        in_specs=[anywhere] * 2,
        out_specs=(anywhere, anywhere),
        scratch_shapes=[
            pltpu.VMEM(outs[0].shape, jnp.bfloat16),
            pltpu.VMEM(outs[1].shape, jnp.bfloat16),
            pltpu.SemaphoreType.DMA((2, 2)),
        ],
        compiler_params=pltpu.CompilerParams(vmem_limit_bytes=56 * 1024 * 1024),
    )(*results)
    return grad_tokens, grad_w[None]


def solution(mesh):
    split = P(("expert", "dp"), None)
    whole = P("expert", None, None)
    return jax.shard_map(
        per_device,
        mesh=mesh,
        in_specs=(split, split, split, split, whole, whole),
        out_specs=(split, P("expert", None, "dp")),
        check_vma=False,
    )
```
